512 devices in a mesh: tensor: 32 (over y_lo, z), dp: 16 (over x, y_hi, core).
Axes of the slice: x: 4, y: 4 (y_hi: 2, y_lo: 2; y = y_hi * 2 + y_lo), z: 16, core: 2. Of those that a mesh axis runs over, the one named last changes fastest.
Arguments:
- hidden: bfloat16 [2048, 4096], P(('dp', 'tensor')), may hold values from -6 to 6
- joined_in: bfloat16 [2048, 8192], P(('dp', 'tensor')), may hold values from -6 to 6
- gate_act: bfloat16 [2048, 28672], P(('dp', 'tensor')), may hold values from -6 to 6
- up_act: bfloat16 [2048, 28672], P(('dp', 'tensor')), may hold values from -6 to 6
- product_grad: bfloat16 [2048, 28672], P(('dp', 'tensor')), may hold values from -6 to 6
- resid_grad: bfloat16 [2048, 4096], P(('dp', 'tensor')), may hold values from -6 to 6
- norm_gain: float32 [4096], replicated, may hold values from 0.1 to 1.9
- gate_weight: bfloat16 [28672, 4096], P('tensor', 'dp'), may hold values from -0.09375 to 0.09375
- up_weight: bfloat16 [28672, 4096], P('tensor', 'dp'), may hold values from -0.09375 to 0.09375
- join_weight: bfloat16 [8192, 4096], P('tensor', 'dp'), may hold values from -0.09375 to 0.09375
Outputs:
- joined_grad: bfloat16 [2048, 8192], P(('dp', 'tensor'))
- gate_weight_grad: float32 [28672, 4096], P('tensor', 'dp')
- up_weight_grad: float32 [28672, 4096], P('tensor', 'dp')
- join_weight_grad: float32 [8192, 4096], P('tensor', 'dp')
- gain_grad: float32 [4096], replicated
The draws below stay inside these ranges and needn't reach their ends.
All inputs are finite; a program needn't handle non-finite values.
Results may differ from the reference program's by a relative error of at most 0.0057.
Values may be sent and summed in bfloat16 or wider, within the bound.
No kernel may reach another device: no remote copies, remote signals or barrier semaphores. Data moves between devices by JAX's collectives and lax.ppermute only.
A program may use at most 64 MiB of HBM per device.

```python
import jax
import jax.numpy as jnp
from jax import lax

D = 4096
FF = 28672
TOKENS = 2048


def steps_of(rng, dims, split, low, high):
    gain, own = 1.0, jax.random.fold_in(rng, 6)
    for position, blocks in split:
        steps = jnp.exp(jax.random.uniform(jax.random.fold_in(own, position), (blocks,), jnp.float32, low / len(split), high / len(split)))
        gain = gain * jnp.repeat(steps, dims[position] // blocks).reshape([-1 if axis == position else 1 for axis in range(len(dims))])
    return gain


def bell_draw(key, extent, deviation, reach, cuts=(), kind=jnp.bfloat16):
    factor_of = steps_of(key, extent, cuts, -0.22, 0.18) if cuts else 1.0
    entries = jax.random.normal(key, extent, jnp.float32) * deviation * factor_of
    return jnp.minimum(jnp.maximum(entries, -reach), reach).astype(kind)


def setup_inputs(seed: int = 0) -> dict:
    streams_of = jax.random.split(jax.random.key(seed), 11)
    return {
        "hidden": bell_draw(streams_of[0], (TOKENS, D), 1.0, 6.0, ((0, 512),)),
        "joined_in": bell_draw(streams_of[1], (TOKENS, 2 * D), 1.0, 6.0, ((0, 512),)),
        "gate_act": bell_draw(streams_of[2], (TOKENS, FF), 1.5, 6.0, ((0, 512),)),
        "up_act": bell_draw(streams_of[3], (TOKENS, FF), 1.0, 6.0, ((0, 512),)),
        "product_grad": bell_draw(streams_of[4], (TOKENS, FF), 1.0, 6.0, ((0, 512),)),
        "resid_grad": bell_draw(streams_of[5], (TOKENS, D), 1.0, 6.0, ((0, 512),)),
        "norm_gain": jnp.clip(1.0 + 0.18 * jax.random.normal(streams_of[6], (D,), jnp.float32), 0.1, 1.9),
        "gate_weight": bell_draw(streams_of[7], (FF, D), D ** -0.5, 0.09375, ((0, 32), (1, 16))),
        "up_weight": bell_draw(streams_of[8], (FF, D), D ** -0.5, 0.09375, ((0, 32), (1, 16))),
        "join_weight": bell_draw(streams_of[9], (2 * D, D), D ** -0.5, 0.09375, ((0, 32), (1, 16))),
    }


def swiglu_back(gate_act, up_act, product_grad):
    gate_wide = gate_act.astype(jnp.float32)
    logistic = jax.nn.sigmoid(gate_wide)
    product_wide = product_grad.astype(jnp.float32)
    gate_grad = product_wide * up_act.astype(jnp.float32) * logistic * (1.0 + gate_wide * (1.0 - logistic))
    up_grad = product_wide * gate_wide * logistic
    return (gate_grad.astype(jnp.bfloat16), up_grad.astype(jnp.bfloat16))

def reference(hidden, joined_in, gate_act, up_act, product_grad, resid_grad, norm_gain, gate_weight, up_weight, join_weight):
    hidden_wide = hidden.astype(jnp.float32)
    row_scale = lax.rsqrt(lax.optimization_barrier(jnp.mean(hidden_wide * hidden_wide, axis=1, keepdims=True)) + 1e-05)
    normed = hidden_wide * row_scale
    mlp_input = (normed * norm_gain).astype(jnp.bfloat16)
    gate_grad, up_grad = swiglu_back(gate_act, up_act, product_grad)
    gate_weight_grad = jnp.dot(gate_grad.T, mlp_input, preferred_element_type=jnp.float32)
    up_weight_grad = jnp.dot(up_grad.T, mlp_input, preferred_element_type=jnp.float32)
    input_grad = jnp.dot(gate_grad, gate_weight, preferred_element_type=jnp.float32) + jnp.dot(up_grad, up_weight, preferred_element_type=jnp.float32)
    lifted = input_grad * norm_gain
    inner_mean = lax.optimization_barrier(jnp.mean(lifted * normed, axis=1, keepdims=True))
    hidden_grad = (resid_grad.astype(jnp.float32) + row_scale * (lifted - normed * inner_mean)).astype(jnp.bfloat16)
    gain_grad = lax.optimization_barrier(jnp.sum(input_grad * normed, axis=0))
    join_weight_grad = jnp.dot(joined_in.T, hidden_grad, preferred_element_type=jnp.float32)
    joined_grad = jnp.dot(hidden_grad, join_weight.T, preferred_element_type=jnp.float32).astype(jnp.bfloat16)
    return (joined_grad, gate_weight_grad, up_weight_grad, join_weight_grad, gain_grad)
```

```python
import jax
import jax.numpy as jnp
from jax import lax
from jax.sharding import Mesh
from jax.sharding import PartitionSpec as P

epsilon = 1e-05
narrow = jnp.bfloat16
wide = jnp.float32


def swiglu_back(gate_act, up_act, product_grad):
    gate_wide = gate_act.astype(wide)
    logistic = jax.nn.sigmoid(gate_wide)
    product_wide = product_grad.astype(wide)
    gate_grad = (
        product_wide * up_act.astype(wide) * logistic * (1.0 + gate_wide * (1.0 - logistic))
    )
    up_grad = product_wide * gate_wide * logistic
    return (gate_grad.astype(narrow), up_grad.astype(narrow))


def token_sum(left, right):
    return lax.dot_general(left, right, (((0,), (0,)), ((), ())), preferred_element_type=wide)


def exchange(blocks, axes):
    return lax.all_to_all(blocks, axes, split_axis=0, concat_axis=0, tiled=True)


def swap_cores(value):
    return lax.ppermute(value, "core", [(0, 1), (1, 0)])


def split_three(value):
    high = value.astype(narrow)
    rest = value - high.astype(wide)
    middle = rest.astype(narrow)
    low = (rest - middle.astype(wide)).astype(narrow)
    return (high, middle, low)


def shards(
    hidden,
    joined_in,
    gate_act,
    up_act,
    product_grad,
    resid_grad,
    norm_gain,
    gate_weight,
    up_weight,
    join_weight,
):
    tensor_axes = ("y_lo", "z")
    dp_axes = ("x", "y_hi", "core")
    z_count = lax.axis_size("z")
    tensor_count = lax.axis_size("y_lo") * z_count
    core_count = lax.axis_size("core")
    dp_count = lax.axis_size("x") * lax.axis_size("y_hi") * core_count
    row_count, width = hidden.shape
    units, features = gate_weight.shape
    inputs = join_weight.shape[0]
    half_inputs = inputs // 2
    group_rows = tensor_count * row_count
    block_rows = dp_count * row_count
    tokens = dp_count * group_rows
    on_first = lax.axis_index("core") == 0

    weight_kept = jnp.where(on_first, gate_weight, up_weight)
    weight_other = swap_cores(jnp.where(on_first, up_weight, gate_weight))
    weight_pair = jnp.concatenate(
        [
            jnp.where(on_first, weight_kept, weight_other),
            jnp.where(on_first, weight_other, weight_kept),
        ],
        axis=1,
    )

    hidden_wide = hidden.astype(wide)
    row_scale = lax.rsqrt(jnp.mean(hidden_wide * hidden_wide, axis=1, keepdims=True) + epsilon)
    scale_parts = jnp.concatenate(split_three(row_scale), axis=1)
    scale_parts = jnp.pad(scale_parts, ((0, 0), (0, features - scale_parts.shape[1])))
    norm_rows = jnp.stack(
        [
            hidden.reshape(row_count, dp_count, features),
            resid_grad.reshape(row_count, dp_count, features),
            jnp.broadcast_to(scale_parts[:, None, :], (row_count, dp_count, features)),
        ]
    )
    norm_block = exchange(norm_rows.transpose(2, 0, 1, 3), dp_axes)
    hidden_block = norm_block[:, 0].reshape(block_rows, features).astype(wide)
    resid_block = norm_block[:, 1].reshape(block_rows, features).astype(wide)
    scale_block = norm_block[:, 2, :, :3].astype(wide).reshape(block_rows, 3)
    scale_block = (scale_block[:, 0:1] + scale_block[:, 1:2]) + scale_block[:, 2:3]
    gain_block = lax.dynamic_slice_in_dim(
        norm_gain, lax.axis_index(dp_axes) * features, features, 0
    )
    normed = hidden_block * scale_block
    mlp_block = (normed * gain_block).astype(narrow)
    mlp_all = lax.all_gather(mlp_block, tensor_axes, axis=0, tiled=True)
    mlp_all = (
        mlp_all.reshape(tensor_count, dp_count, row_count, features)
        .transpose(1, 0, 2, 3)
        .reshape(tokens, features)
    )
    mlp_other = swap_cores(mlp_all)
    mlp_pair = jnp.concatenate(
        [jnp.where(on_first, mlp_all, mlp_other), jnp.where(on_first, mlp_other, mlp_all)],
        axis=1,
    )

    gate_grad, up_grad = swiglu_back(gate_act, up_act, product_grad)
    joined_rows = joined_in.reshape(row_count, tensor_count, 2, half_inputs)
    half_width = units + half_inputs
    gate_rows = jnp.concatenate(
        [gate_grad.reshape(row_count, tensor_count, units), joined_rows[:, :, 0]], axis=2
    )
    up_rows = jnp.concatenate(
        [up_grad.reshape(row_count, tensor_count, units), joined_rows[:, :, 1]], axis=2
    )
    unit_rows = jnp.stack([gate_rows, up_rows]).transpose(2, 0, 1, 3)
    unit_group = exchange(
        unit_rows.reshape(tensor_count, 2 * row_count, half_width), tensor_axes
    )
    unit_halves = (
        unit_group.reshape(tensor_count, 2, row_count, half_width)
        .transpose(1, 0, 2, 3)
        .reshape(2, group_rows, half_width)
    )
    unit_halves = jnp.broadcast_to(
        unit_halves[None], (dp_count // core_count, core_count, group_rows, half_width)
    ).reshape(dp_count, group_rows, half_width)
    half_all = exchange(unit_halves, dp_axes).reshape(tokens, half_width)
    grad_half = half_all[:, :units]
    joined_half = half_all[:, units:]

    partial_value = jnp.dot(grad_half, weight_pair, preferred_element_type=wide).astype(narrow)
    partial_value = partial_value.reshape(
        dp_count, 2, z_count, row_count, core_count, features
    ).transpose(1, 4, 2, 0, 3, 5)
    near = exchange(
        partial_value.reshape(2 * core_count, z_count * block_rows, features), ("y_lo", "core")
    )
    near_sum = jnp.sum(near.astype(wide), axis=0).astype(narrow)
    far = exchange(near_sum.reshape(z_count, block_rows, features), "z")
    input_grad = jnp.sum(far.astype(wide), axis=0)

    lifted = input_grad * gain_block
    mean_part = jnp.sum(lifted * normed, axis=1)
    mean_all = exchange(
        jnp.broadcast_to(mean_part[None, None], (dp_count, 1, block_rows)), dp_axes
    )
    inner_mean = (jnp.sum(mean_all, axis=(0, 1)) / width)[:, None]
    hidden_grad = (resid_block + scale_block * (lifted - normed * inner_mean)).astype(narrow)
    gain_part = jnp.sum(input_grad * normed, axis=0, keepdims=True)
    gain_parts = lax.all_gather(gain_part, tensor_axes, axis=0, tiled=True)
    gain_sum = jnp.sum(gain_parts, axis=0, keepdims=True)

    grad_far = exchange(
        jnp.broadcast_to(hidden_grad[None], (z_count, block_rows, features)), "z"
    ).reshape(1, z_count * block_rows, features)
    grad_all = exchange(
        jnp.broadcast_to(grad_far, (2, z_count * block_rows, features)), "y_lo"
    )
    grad_all = (
        grad_all.reshape(tensor_count, dp_count, row_count, features)
        .transpose(1, 0, 2, 3)
        .reshape(tokens, features)
    )
    joined_part = lax.dot_general(
        grad_all, join_weight, (((1,), (1,)), ((), ())), preferred_element_type=wide
    ).astype(narrow)
    gain_rows = jnp.concatenate(
        list(split_three(gain_sum)) + [jnp.zeros((13, features), narrow)], axis=0
    )
    joined_part = jnp.concatenate(
        [
            joined_part.reshape(dp_count, group_rows, inputs),
            jnp.broadcast_to(gain_rows[None], (dp_count, 16, features)),
        ],
        axis=1,
    )
    joined_blocks = exchange(joined_part, dp_axes)
    gain_grad = joined_blocks[:, group_rows : group_rows + 3].astype(wide)
    gain_grad = ((gain_grad[:, 0] + gain_grad[:, 1]) + gain_grad[:, 2]).reshape(width)
    joined_total = jnp.sum(joined_blocks[:, :group_rows].astype(wide), axis=0).astype(narrow)
    joined_grad = exchange(joined_total.reshape(tensor_count, row_count, inputs), tensor_axes)
    joined_grad = joined_grad.transpose(1, 0, 2).reshape(row_count, tensor_count * inputs)

    unit_weight_grad = token_sum(grad_half, mlp_pair)
    grad_first = unit_weight_grad[:, :features]
    grad_second = unit_weight_grad[:, features:]
    own_grad = jnp.where(on_first, grad_first, grad_second)
    other_grad = swap_cores(jnp.where(on_first, grad_second, grad_first))
    gate_weight_grad = jnp.where(on_first, own_grad, other_grad)
    up_weight_grad = jnp.where(on_first, other_grad, own_grad)
    joined_other = swap_cores(joined_half)
    joined_all = jnp.concatenate(
        [
            jnp.where(on_first, joined_half, joined_other),
            jnp.where(on_first, joined_other, joined_half),
        ],
        axis=1,
    )
    join_weight_grad = token_sum(joined_all, grad_all)
    return (joined_grad, gate_weight_grad, up_weight_grad, join_weight_grad, gain_grad)


def solution(mesh):
    tensor_count, dp_count = mesh.shape["tensor"], mesh.shape["dp"]
    fine = Mesh(
        mesh.devices.reshape(2, tensor_count // 2, dp_count // 4, 2, 2),
        ("y_lo", "z", "x", "y_hi", "core"),
    )
    tensor_axes = ("y_lo", "z")
    dp_axes = ("x", "y_hi", "core")
    rows = P(dp_axes + tensor_axes, None)
    blocks = P(tensor_axes, dp_axes)
    in_specs = (rows, rows, rows, rows, rows, rows, P(), blocks, blocks, blocks)
    out_specs = (rows, blocks, blocks, blocks, P())
    return jax.shard_map(shards, mesh=fine, in_specs=in_specs, out_specs=out_specs, check_vma=False)
```

```python
import jax
import jax.numpy as jnp
from jax import lax
from jax.sharding import Mesh
from jax.sharding import PartitionSpec as P

epsilon = 1e-05
narrow = jnp.bfloat16
wide = jnp.float32


def swiglu_back(gate_act, up_act, product_grad):
    gate_wide = gate_act.astype(wide)
    logistic = jax.nn.sigmoid(gate_wide)
    product_wide = product_grad.astype(wide)
    gate_grad = (
        product_wide * up_act.astype(wide) * logistic * (1.0 + gate_wide * (1.0 - logistic))
    )
    up_grad = product_wide * gate_wide * logistic
    return (gate_grad.astype(narrow), up_grad.astype(narrow))


def token_sum(left, right):
    return lax.dot_general(left, right, (((0,), (0,)), ((), ())), preferred_element_type=wide)


def exchange(blocks, axes):
    return lax.all_to_all(blocks, axes, split_axis=0, concat_axis=0, tiled=True)


def swap_cores(value):
    return lax.ppermute(value, "core", [(0, 1), (1, 0)])


def swap_near(value):
    return lax.ppermute(value, "y_lo", [(0, 1), (1, 0)])


def split_three(value):
    high = value.astype(narrow)
    rest = value - high.astype(wide)
    middle = rest.astype(narrow)
    low = (rest - middle.astype(wide)).astype(narrow)
    return (high, middle, low)


def shards(
    hidden,
    joined_in,
    gate_act,
    up_act,
    product_grad,
    resid_grad,
    norm_gain,
    gate_weight,
    up_weight,
    join_weight,
):
    tensor_axes = ("y_lo", "z")
    dp_axes = ("x", "y_hi", "core")
    z_count = lax.axis_size("z")
    tensor_count = lax.axis_size("y_lo") * z_count
    core_count = lax.axis_size("core")
    dp_count = lax.axis_size("x") * lax.axis_size("y_hi") * core_count
    row_count, width = hidden.shape
    units, features = gate_weight.shape
    inputs = join_weight.shape[0]
    half_inputs = inputs // 2
    group_rows = tensor_count * row_count
    block_rows = dp_count * row_count
    tokens = dp_count * group_rows
    on_first = lax.axis_index("core") == 0

    weight_kept = jnp.where(on_first, gate_weight, up_weight)
    weight_other = swap_cores(jnp.where(on_first, up_weight, gate_weight))

    hidden_wide = hidden.astype(wide)
    row_scale = lax.rsqrt(jnp.mean(hidden_wide * hidden_wide, axis=1, keepdims=True) + epsilon)
    scale_parts = jnp.concatenate(split_three(row_scale), axis=1)
    scale_parts = jnp.pad(scale_parts, ((0, 0), (0, features - scale_parts.shape[1])))
    norm_rows = jnp.stack(
        [
            hidden.reshape(row_count, dp_count, features),
            resid_grad.reshape(row_count, dp_count, features),
            jnp.broadcast_to(scale_parts[:, None, :], (row_count, dp_count, features)),
        ]
    )
    norm_block = exchange(norm_rows.transpose(2, 0, 1, 3), dp_axes)
    hidden_block = norm_block[:, 0].reshape(block_rows, features).astype(wide)
    resid_block = norm_block[:, 1].reshape(block_rows, features).astype(wide)
    scale_block = norm_block[:, 2, :, :3].astype(wide).reshape(block_rows, 3)
    scale_block = (scale_block[:, 0:1] + scale_block[:, 1:2]) + scale_block[:, 2:3]
    gain_block = lax.dynamic_slice_in_dim(
        norm_gain, lax.axis_index(dp_axes) * features, features, 0
    )
    normed = hidden_block * scale_block
    mlp_block = (normed * gain_block).astype(narrow)

    gate_grad, up_grad = swiglu_back(gate_act, up_act, product_grad)
    joined_rows = joined_in.reshape(row_count, tensor_count, 2, half_inputs)
    half_width = units + half_inputs
    gate_rows = jnp.concatenate(
        [gate_grad.reshape(row_count, tensor_count, units), joined_rows[:, :, 0]], axis=2
    )
    up_rows = jnp.concatenate(
        [up_grad.reshape(row_count, tensor_count, units), joined_rows[:, :, 1]], axis=2
    )
    unit_rows = jnp.stack([gate_rows, up_rows]).transpose(2, 0, 1, 3)
    unit_rows, mlp_sent = lax.optimization_barrier((unit_rows, mlp_block))
    unit_group = exchange(
        unit_rows.reshape(tensor_count, 2 * row_count, half_width), tensor_axes
    )
    mlp_all = lax.all_gather(mlp_sent, tensor_axes, axis=0, tiled=True)
    mlp_all = (
        mlp_all.reshape(tensor_count, dp_count, row_count, features)
        .transpose(1, 0, 2, 3)
        .reshape(tokens, features)
    )
    mlp_other = swap_cores(mlp_all)
    unit_halves = (
        unit_group.reshape(tensor_count, 2, row_count, half_width)
        .transpose(1, 0, 2, 3)
        .reshape(2, group_rows, half_width)
    )
    unit_halves = jnp.broadcast_to(
        unit_halves[None], (dp_count // core_count, core_count, group_rows, half_width)
    ).reshape(dp_count, group_rows, half_width)
    half_all = exchange(unit_halves, dp_axes).reshape(tokens, half_width)
    grad_half = half_all[:, :units]
    joined_half = half_all[:, units:]

    partial_other = jnp.dot(grad_half, weight_other, preferred_element_type=wide)
    partial_own = jnp.dot(grad_half, weight_kept, preferred_element_type=wide)
    partial_value = (partial_own + swap_cores(partial_other)).reshape(
        dp_count, 2, z_count * row_count, features
    )
    here = lax.axis_index("y_lo")
    near_kept = lax.dynamic_index_in_dim(partial_value, here, 1, keepdims=False)
    near_sent = lax.dynamic_index_in_dim(partial_value, 1 - here, 1, keepdims=False)
    near_sum = near_kept + swap_near(near_sent.astype(narrow)).astype(wide)
    near_sum = (
        near_sum.astype(narrow)
        .reshape(dp_count, z_count, row_count, features)
        .transpose(1, 0, 2, 3)
        .reshape(z_count, block_rows, features)
    )
    far = exchange(near_sum, "z")
    input_grad = jnp.sum(far.astype(wide), axis=0)

    lifted = input_grad * gain_block
    mean_part = jnp.sum(lifted * normed, axis=1)
    mean_all = exchange(
        jnp.broadcast_to(mean_part[None, None], (dp_count, 1, block_rows)), dp_axes
    )
    inner_mean = (jnp.sum(mean_all, axis=(0, 1)) / width)[:, None]
    hidden_grad = (resid_block + scale_block * (lifted - normed * inner_mean)).astype(narrow)
    gain_part = jnp.sum(input_grad * normed, axis=0, keepdims=True)

    sent_rows = block_rows + 8
    grad_sent = jnp.concatenate(
        [hidden_grad] + list(split_three(gain_part)) + [jnp.zeros((5, features), narrow)], axis=0
    )
    grad_far = exchange(jnp.broadcast_to(grad_sent[None], (z_count, sent_rows, features)), "z")
    grad_near = swap_near(grad_far)
    grad_pair = jnp.stack(
        [jnp.where(here == 0, grad_far, grad_near), jnp.where(here == 0, grad_near, grad_far)]
    )
    gain_parts = grad_pair[:, :, block_rows : block_rows + 3].astype(wide)
    gain_sum = jnp.sum(gain_parts, axis=(0, 1, 2))[None]
    grad_all = (
        grad_pair[:, :, :block_rows]
        .reshape(tensor_count, dp_count, row_count, features)
        .transpose(1, 0, 2, 3)
        .reshape(tokens, features)
    )
    joined_part = lax.dot_general(
        grad_all, join_weight, (((1,), (1,)), ((), ())), preferred_element_type=wide
    ).astype(narrow)
    gain_rows = jnp.concatenate(
        list(split_three(gain_sum)) + [jnp.zeros((13, features), narrow)], axis=0
    )
    joined_part = jnp.concatenate(
        [
            joined_part.reshape(dp_count, group_rows, inputs),
            jnp.broadcast_to(gain_rows[None], (dp_count, 16, features)),
        ],
        axis=1,
    )
    joined_blocks = exchange(joined_part, dp_axes)
    gain_grad = joined_blocks[:, group_rows : group_rows + 3].astype(wide)
    gain_grad = ((gain_grad[:, 0] + gain_grad[:, 1]) + gain_grad[:, 2]).reshape(width)
    joined_total = jnp.sum(joined_blocks[:, :group_rows].astype(wide), axis=0).astype(narrow)
    joined_grad = exchange(joined_total.reshape(tensor_count, row_count, inputs), tensor_axes)
    joined_grad = joined_grad.transpose(1, 0, 2).reshape(row_count, tensor_count * inputs)

    kept_grad = token_sum(grad_half, mlp_all)
    other_grad = swap_cores(token_sum(grad_half, mlp_other))
    gate_weight_grad = jnp.where(on_first, kept_grad, other_grad)
    up_weight_grad = jnp.where(on_first, other_grad, kept_grad)
    joined_other = swap_cores(joined_half)
    join_kept = token_sum(joined_half, grad_all)
    join_other = token_sum(joined_other, grad_all)
    join_weight_grad = jnp.concatenate(
        [jnp.where(on_first, join_kept, join_other), jnp.where(on_first, join_other, join_kept)],
        axis=0,
    )
    return (joined_grad, gate_weight_grad, up_weight_grad, join_weight_grad, gain_grad)


def solution(mesh):
    tensor_count, dp_count = mesh.shape["tensor"], mesh.shape["dp"]
    fine = Mesh(
        mesh.devices.reshape(2, tensor_count // 2, dp_count // 4, 2, 2),
        ("y_lo", "z", "x", "y_hi", "core"),
    )
    tensor_axes = ("y_lo", "z")
    dp_axes = ("x", "y_hi", "core")
    rows = P(dp_axes + tensor_axes, None)
    blocks = P(tensor_axes, dp_axes)
    in_specs = (rows, rows, rows, rows, rows, rows, P(), blocks, blocks, blocks)
    out_specs = (rows, blocks, blocks, blocks, P())
    return jax.shard_map(shards, mesh=fine, in_specs=in_specs, out_specs=out_specs, check_vma=False)
```

```python
import jax
import jax.numpy as jnp
from jax import lax
from jax.sharding import Mesh
from jax.sharding import PartitionSpec as P

epsilon = 1e-05
narrow = jnp.bfloat16
wide = jnp.float32


def swiglu_back(gate_act, up_act, product_grad):
    gate_wide = gate_act.astype(wide)
    logistic = jax.nn.sigmoid(gate_wide)
    product_wide = product_grad.astype(wide)
    gate_grad = (
        product_wide * up_act.astype(wide) * logistic * (1.0 + gate_wide * (1.0 - logistic))
    )
    up_grad = product_wide * gate_wide * logistic
    return (gate_grad.astype(narrow), up_grad.astype(narrow))


def token_sum(left, right):
    return lax.dot_general(left, right, (((0,), (0,)), ((), ())), preferred_element_type=wide)


def exchange(blocks, axes):
    return lax.all_to_all(blocks, axes, split_axis=0, concat_axis=0, tiled=True)


def swap_cores(value):
    return lax.ppermute(value, "core", [(0, 1), (1, 0)])


def swap_near(value):
    return lax.ppermute(value, "y_lo", [(0, 1), (1, 0)])


def from_above(value, distance):
    count = lax.axis_size("z")
    return lax.ppermute(value, "z", [((i + distance) % count, i) for i in range(count)])


def gather_blocks(block):
    near = swap_near(block)
    first = lax.axis_index("y_lo") == 0
    pair = jnp.stack([jnp.where(first, block, near), jnp.where(first, near, block)])
    z_count = lax.axis_size("z")
    quarter = z_count // 4
    strided = jnp.stack([pair] + [from_above(pair, 4 * step) for step in range(1, quarter)])
    below = from_above(strided, z_count - 1)
    below = jnp.concatenate([below[1:], below[:1]])
    all_pairs = jnp.stack(
        [strided, from_above(strided, 1), from_above(strided, 2), below], axis=1
    ).reshape(z_count, *pair.shape)
    twice = jnp.concatenate([all_pairs, all_pairs])
    return lax.dynamic_slice_in_dim(twice, z_count - lax.axis_index("z"), z_count, 0)


def split_three(value):
    high = value.astype(narrow)
    rest = value - high.astype(wide)
    middle = rest.astype(narrow)
    low = (rest - middle.astype(wide)).astype(narrow)
    return (high, middle, low)


def shards(
    hidden,
    joined_in,
    gate_act,
    up_act,
    product_grad,
    resid_grad,
    norm_gain,
    gate_weight,
    up_weight,
    join_weight,
):
    tensor_axes = ("y_lo", "z")
    dp_axes = ("x", "y_hi", "core")
    z_count = lax.axis_size("z")
    tensor_count = lax.axis_size("y_lo") * z_count
    core_count = lax.axis_size("core")
    dp_count = lax.axis_size("x") * lax.axis_size("y_hi") * core_count
    row_count, width = hidden.shape
    units, features = gate_weight.shape
    inputs = join_weight.shape[0]
    half_inputs = inputs // 2
    group_rows = tensor_count * row_count
    block_rows = dp_count * row_count
    tokens = dp_count * group_rows
    on_first = lax.axis_index("core") == 0

    weight_kept = jnp.where(on_first, gate_weight, up_weight)
    weight_other = swap_cores(jnp.where(on_first, up_weight, gate_weight))

    hidden_wide = hidden.astype(wide)
    row_scale = lax.rsqrt(jnp.mean(hidden_wide * hidden_wide, axis=1, keepdims=True) + epsilon)
    scale_parts = jnp.concatenate(split_three(row_scale), axis=1)
    scale_parts = jnp.pad(scale_parts, ((0, 0), (0, features - scale_parts.shape[1])))
    norm_rows = jnp.stack(
        [
            hidden.reshape(row_count, dp_count, features),
            resid_grad.reshape(row_count, dp_count, features),
            jnp.broadcast_to(scale_parts[:, None, :], (row_count, dp_count, features)),
        ]
    )
    norm_block = exchange(norm_rows.transpose(2, 0, 1, 3), dp_axes)
    hidden_block = norm_block[:, 0].reshape(block_rows, features).astype(wide)
    resid_block = norm_block[:, 1].reshape(block_rows, features).astype(wide)
    scale_block = norm_block[:, 2, :, :3].astype(wide).reshape(block_rows, 3)
    scale_block = (scale_block[:, 0:1] + scale_block[:, 1:2]) + scale_block[:, 2:3]
    gain_block = lax.dynamic_slice_in_dim(
        norm_gain, lax.axis_index(dp_axes) * features, features, 0
    )
    normed = hidden_block * scale_block
    mlp_block = (normed * gain_block).astype(narrow)

    gate_grad, up_grad = swiglu_back(gate_act, up_act, product_grad)
    joined_rows = joined_in.reshape(row_count, tensor_count, 2, half_inputs)
    half_width = units + half_inputs
    gate_rows = jnp.concatenate(
        [gate_grad.reshape(row_count, tensor_count, units), joined_rows[:, :, 0]], axis=2
    )
    up_rows = jnp.concatenate(
        [up_grad.reshape(row_count, tensor_count, units), joined_rows[:, :, 1]], axis=2
    )
    unit_rows = jnp.stack([gate_rows, up_rows]).transpose(2, 0, 1, 3)
    unit_group = exchange(
        unit_rows.reshape(tensor_count, 2 * row_count, half_width), tensor_axes
    )
    mlp_all = gather_blocks(mlp_block)
    unit_halves = (
        unit_group.reshape(tensor_count, 2, row_count, half_width)
        .transpose(1, 0, 2, 3)
        .reshape(2, group_rows, half_width)
    )
    unit_halves = jnp.broadcast_to(
        unit_halves[None], (dp_count // core_count, core_count, group_rows, half_width)
    ).reshape(dp_count, group_rows, half_width)
    half_all = exchange(unit_halves, dp_axes).reshape(tokens, half_width)
    half_all, mlp_all = lax.optimization_barrier((half_all, mlp_all))
    mlp_all = (
        mlp_all.reshape(z_count, 2, dp_count, row_count, features)
        .transpose(2, 1, 0, 3, 4)
        .reshape(tokens, features)
    )
    mlp_other = swap_cores(mlp_all)
    grad_half = half_all[:, :units]
    joined_half = half_all[:, units:]

    partial_other = jnp.dot(grad_half, weight_other, preferred_element_type=wide)
    partial_own = jnp.dot(grad_half, weight_kept, preferred_element_type=wide)
    partial_value = (partial_own + swap_cores(partial_other)).reshape(
        dp_count, 2, z_count * row_count, features
    )
    here = lax.axis_index("y_lo")
    near_kept = lax.dynamic_index_in_dim(partial_value, here, 1, keepdims=False)
    near_sent = lax.dynamic_index_in_dim(partial_value, 1 - here, 1, keepdims=False)
    near_sum = near_kept + swap_near(near_sent.astype(narrow)).astype(wide)
    near_sum = (
        near_sum.astype(narrow)
        .reshape(dp_count, z_count, row_count, features)
        .transpose(1, 0, 2, 3)
        .reshape(z_count, block_rows, features)
    )
    far = exchange(near_sum, "z")
    input_grad = jnp.sum(far.astype(wide), axis=0)

    lifted = input_grad * gain_block
    mean_part = jnp.sum(lifted * normed, axis=1)
    mean_all = exchange(
        jnp.broadcast_to(mean_part[None, None], (dp_count, 1, block_rows)), dp_axes
    )
    inner_mean = (jnp.sum(mean_all, axis=(0, 1)) / width)[:, None]
    hidden_grad = (resid_block + scale_block * (lifted - normed * inner_mean)).astype(narrow)
    gain_part = jnp.sum(input_grad * normed, axis=0, keepdims=True)

    sent_rows = block_rows + 8
    grad_sent = jnp.concatenate(
        [hidden_grad] + list(split_three(gain_part)) + [jnp.zeros((5, features), narrow)], axis=0
    )
    grad_far = exchange(jnp.broadcast_to(grad_sent[None], (z_count, sent_rows, features)), "z")
    grad_near = swap_near(grad_far)
    grad_pair = jnp.stack(
        [jnp.where(here == 0, grad_far, grad_near), jnp.where(here == 0, grad_near, grad_far)]
    )
    gain_parts = grad_pair[:, :, block_rows : block_rows + 3].astype(wide)
    gain_sum = jnp.sum(gain_parts, axis=(0, 1, 2))[None]
    grad_all = (
        grad_pair[:, :, :block_rows]
        .reshape(tensor_count, dp_count, row_count, features)
        .transpose(1, 0, 2, 3)
        .reshape(tokens, features)
    )
    joined_part = lax.dot_general(
        grad_all, join_weight, (((1,), (1,)), ((), ())), preferred_element_type=wide
    ).astype(narrow)
    gain_rows = jnp.concatenate(
        list(split_three(gain_sum)) + [jnp.zeros((13, features), narrow)], axis=0
    )
    joined_part = jnp.concatenate(
        [
            joined_part.reshape(dp_count, group_rows, inputs),
            jnp.broadcast_to(gain_rows[None], (dp_count, 16, features)),
        ],
        axis=1,
    )
    joined_blocks = exchange(joined_part, dp_axes)
    gain_grad = joined_blocks[:, group_rows : group_rows + 3].astype(wide)
    gain_grad = ((gain_grad[:, 0] + gain_grad[:, 1]) + gain_grad[:, 2]).reshape(width)
    joined_total = jnp.sum(joined_blocks[:, :group_rows].astype(wide), axis=0).astype(narrow)
    joined_grad = exchange(joined_total.reshape(tensor_count, row_count, inputs), tensor_axes)
    joined_grad = joined_grad.transpose(1, 0, 2).reshape(row_count, tensor_count * inputs)

    kept_grad = token_sum(grad_half, mlp_all)
    other_grad = swap_cores(token_sum(grad_half, mlp_other))
    gate_weight_grad = jnp.where(on_first, kept_grad, other_grad)
    up_weight_grad = jnp.where(on_first, other_grad, kept_grad)
    joined_other = swap_cores(joined_half)
    join_kept = token_sum(joined_half, grad_all)
    join_other = token_sum(joined_other, grad_all)
    join_weight_grad = jnp.concatenate(
        [jnp.where(on_first, join_kept, join_other), jnp.where(on_first, join_other, join_kept)],
        axis=0,
    )
    return (joined_grad, gate_weight_grad, up_weight_grad, join_weight_grad, gain_grad)


def solution(mesh):
    tensor_count, dp_count = mesh.shape["tensor"], mesh.shape["dp"]
    fine = Mesh(
        mesh.devices.reshape(2, tensor_count // 2, dp_count // 4, 2, 2),
        ("y_lo", "z", "x", "y_hi", "core"),
    )
    tensor_axes = ("y_lo", "z")
    dp_axes = ("x", "y_hi", "core")
    rows = P(dp_axes + tensor_axes, None)
    blocks = P(tensor_axes, dp_axes)
    in_specs = (rows, rows, rows, rows, rows, rows, P(), blocks, blocks, blocks)
    out_specs = (rows, blocks, blocks, blocks, P())
    return jax.shard_map(shards, mesh=fine, in_specs=in_specs, out_specs=out_specs, check_vma=False)
```

```python
import jax
import jax.numpy as jnp
from jax import lax
from jax.sharding import Mesh
from jax.sharding import PartitionSpec as P

epsilon = 1e-05
narrow = jnp.bfloat16
wide = jnp.float32


def swiglu_back(gate_act, up_act, product_grad):
    gate_wide = gate_act.astype(wide)
    logistic = jax.nn.sigmoid(gate_wide)
    product_wide = product_grad.astype(wide)
    gate_grad = (
        product_wide * up_act.astype(wide) * logistic * (1.0 + gate_wide * (1.0 - logistic))
    )
    up_grad = product_wide * gate_wide * logistic
    return (gate_grad.astype(narrow), up_grad.astype(narrow))


def token_sum(left, right):
    return lax.dot_general(left, right, (((0,), (0,)), ((), ())), preferred_element_type=wide)


def exchange(blocks, axes):
    return lax.all_to_all(blocks, axes, split_axis=0, concat_axis=0, tiled=True)


def swap_cores(value):
    return lax.ppermute(value, "core", [(0, 1), (1, 0)])


def swap_near(value):
    return lax.ppermute(value, "y_lo", [(0, 1), (1, 0)])


def from_above(value, distance):
    count = lax.axis_size("z")
    return lax.ppermute(value, "z", [((i + distance) % count, i) for i in range(count)])


def gather_z(block):
    z_count = lax.axis_size("z")
    quarter = z_count // 4
    strided = jnp.stack([block] + [from_above(block, 4 * step) for step in range(1, quarter)])
    below = from_above(strided, z_count - 1)
    below = jnp.concatenate([below[1:], below[:1]])
    all_blocks = jnp.stack(
        [strided, from_above(strided, 1), from_above(strided, 2), below], axis=1
    ).reshape(z_count, *block.shape)
    twice = jnp.concatenate([all_blocks, all_blocks])
    return lax.dynamic_slice_in_dim(twice, z_count - lax.axis_index("z"), z_count, 0)


def trade_pair(blocks, axis_name):
    first = lax.axis_index(axis_name) == 0
    kept = jnp.where(first, blocks[0], blocks[1])
    sent = jnp.where(first, blocks[1], blocks[0])
    other = lax.ppermute(sent, axis_name, [(0, 1), (1, 0)])
    return jnp.stack([jnp.where(first, kept, other), jnp.where(first, other, kept)])


def trade_x(blocks):
    count, here = lax.axis_size("x"), lax.axis_index("x")
    turned = lax.dynamic_slice_in_dim(jnp.concatenate([blocks, blocks]), here, count, 0)
    pieces = [turned[0]] + [
        lax.ppermute(turned[step], "x", [(i, (i + step) % count) for i in range(count)])
        for step in range(1, count)
    ]
    back = jnp.stack([pieces[(count - step) % count] for step in range(count)])
    return lax.dynamic_slice_in_dim(jnp.concatenate([back, back]), count - here, count, 0)


def other_first(pair):
    return jnp.where(lax.axis_index("y_lo") == 0, pair[::-1], pair)


def split_three(value):
    high = value.astype(narrow)
    rest = value - high.astype(wide)
    middle = rest.astype(narrow)
    low = (rest - middle.astype(wide)).astype(narrow)
    return (high, middle, low)


def shards(
    hidden,
    joined_in,
    gate_act,
    up_act,
    product_grad,
    resid_grad,
    norm_gain,
    gate_weight,
    up_weight,
    join_weight,
):
    tensor_axes = ("y_lo", "z")
    dp_axes = ("x", "y_hi", "core")
    z_count = lax.axis_size("z")
    tensor_count = lax.axis_size("y_lo") * z_count
    core_count = lax.axis_size("core")
    dp_count = lax.axis_size("x") * lax.axis_size("y_hi") * core_count
    row_count, width = hidden.shape
    units, features = gate_weight.shape
    inputs = join_weight.shape[0]
    half_inputs = inputs // 2
    group_rows = tensor_count * row_count
    block_rows = dp_count * row_count
    tokens = dp_count * group_rows
    on_first = lax.axis_index("core") == 0

    weight_kept = jnp.where(on_first, gate_weight, up_weight)
    weight_other = swap_cores(jnp.where(on_first, up_weight, gate_weight))

    hidden_wide = hidden.astype(wide)
    row_scale = lax.rsqrt(jnp.mean(hidden_wide * hidden_wide, axis=1, keepdims=True) + epsilon)
    scale_parts = jnp.concatenate(split_three(row_scale), axis=1)
    scale_parts = jnp.pad(scale_parts, ((0, 0), (0, features - scale_parts.shape[1])))
    norm_rows = jnp.stack(
        [
            hidden.reshape(row_count, dp_count, features),
            resid_grad.reshape(row_count, dp_count, features),
            jnp.broadcast_to(scale_parts[:, None, :], (row_count, dp_count, features)),
        ]
    )
    norm_sent = norm_rows.transpose(2, 0, 1, 3).reshape(
        lax.axis_size("x"), 2, 2, 3 * row_count, features
    )
    norm_block = trade_pair(norm_sent.transpose(2, 0, 1, 3, 4), "core")
    norm_block = trade_pair(norm_block.transpose(2, 0, 1, 3, 4), "y_hi")
    norm_block = trade_x(norm_block.transpose(2, 0, 1, 3, 4)).reshape(
        dp_count, 3, row_count, features
    )
    hidden_block = norm_block[:, 0].reshape(block_rows, features).astype(wide)
    resid_block = norm_block[:, 1].reshape(block_rows, features).astype(wide)
    scale_block = norm_block[:, 2, :, :3].astype(wide).reshape(block_rows, 3)
    scale_block = (scale_block[:, 0:1] + scale_block[:, 1:2]) + scale_block[:, 2:3]
    gain_block = lax.dynamic_slice_in_dim(
        norm_gain, lax.axis_index(dp_axes) * features, features, 0
    )
    normed = hidden_block * scale_block
    mlp_block = (normed * gain_block).astype(narrow)

    gate_grad, up_grad = swiglu_back(gate_act, up_act, product_grad)
    joined_rows = joined_in.reshape(row_count, tensor_count, 2, half_inputs)
    half_width = units + half_inputs
    gate_rows = jnp.concatenate(
        [gate_grad.reshape(row_count, tensor_count, units), joined_rows[:, :, 0]], axis=2
    )
    up_rows = jnp.concatenate(
        [up_grad.reshape(row_count, tensor_count, units), joined_rows[:, :, 1]], axis=2
    )
    unit_rows = jnp.stack([gate_rows, up_rows]).transpose(2, 0, 1, 3)
    unit_group = exchange(
        unit_rows.reshape(tensor_count, 2 * row_count, half_width), tensor_axes
    )
    unit_group, mlp_block = lax.optimization_barrier((unit_group, mlp_block))
    mlp_z = gather_z(mlp_block)
    unit_halves = (
        other_first(unit_group.reshape(2, z_count, 2, row_count, half_width))
        .transpose(2, 0, 1, 3, 4)
        .reshape(2, group_rows, half_width)
    )
    unit_halves = jnp.broadcast_to(
        unit_halves[None], (dp_count // core_count, core_count, group_rows, half_width)
    ).reshape(dp_count, group_rows, half_width)
    half_all = exchange(unit_halves, dp_axes).reshape(tokens, half_width)
    half_all, mlp_z = lax.optimization_barrier((half_all, mlp_z))
    mlp_all = (
        jnp.stack([swap_near(mlp_z), mlp_z])
        .reshape(2, z_count, dp_count, row_count, features)
        .transpose(2, 0, 1, 3, 4)
        .reshape(tokens, features)
    )
    mlp_other = swap_cores(mlp_all)
    grad_half = half_all[:, :units]
    joined_half = half_all[:, units:]

    sent_rows, kept_rows = (
        half_all.reshape(dp_count, 2, z_count * row_count, half_width)[:, side].reshape(
            -1, half_width
        )
        for side in range(2)
    )
    weight_other, weight_kept = (
        jnp.pad(weight, ((0, half_width - units), (0, 0)))
        for weight in (weight_other, weight_kept)
    )
    sent_other = swap_cores(jnp.dot(sent_rows, weight_other, preferred_element_type=wide))
    sent_own = jnp.dot(sent_rows, weight_kept, preferred_element_type=wide)
    near_part = swap_near((sent_own + sent_other).astype(narrow))
    kept_other = swap_cores(jnp.dot(kept_rows, weight_other, preferred_element_type=wide))
    kept_own = jnp.dot(kept_rows, weight_kept, preferred_element_type=wide)
    near_sum = kept_own + kept_other + near_part.astype(wide)
    near_sum = (
        near_sum.astype(narrow)
        .reshape(dp_count, z_count, row_count, features)
        .transpose(1, 0, 2, 3)
        .reshape(z_count, block_rows, features)
    )
    far = exchange(near_sum, "z")
    input_grad = jnp.sum(far.astype(wide), axis=0)

    lifted = input_grad * gain_block
    mean_part = jnp.sum(lifted * normed, axis=1)
    mean_all = exchange(
        jnp.broadcast_to(mean_part[None, None], (dp_count, 1, block_rows)), dp_axes
    )
    inner_mean = (jnp.sum(mean_all, axis=(0, 1)) / width)[:, None]
    hidden_grad = (resid_block + scale_block * (lifted - normed * inner_mean)).astype(narrow)
    gain_part = jnp.sum(input_grad * normed, axis=0, keepdims=True)

    rows_sent = block_rows + 8
    grad_sent = jnp.concatenate(
        [hidden_grad] + list(split_three(gain_part)) + [jnp.zeros((5, features), narrow)], axis=0
    )
    grad_far = exchange(jnp.broadcast_to(grad_sent[None], (z_count, rows_sent, features)), "z")
    grad_near = swap_near(grad_far)
    grad_pair = jnp.stack([grad_near, grad_far])
    gain_parts = grad_pair[:, :, block_rows : block_rows + 3].astype(wide)
    gain_sum = jnp.sum(gain_parts, axis=(0, 1, 2))[None]
    grad_all = (
        grad_pair[:, :, :block_rows]
        .reshape(tensor_count, dp_count, row_count, features)
        .transpose(1, 0, 2, 3)
        .reshape(tokens, features)
    )
    joined_part = lax.dot_general(
        grad_all, join_weight, (((1,), (1,)), ((), ())), preferred_element_type=wide
    ).astype(narrow)
    gain_rows = jnp.concatenate(
        list(split_three(gain_sum)) + [jnp.zeros((13, features), narrow)], axis=0
    )
    joined_part = jnp.concatenate(
        [
            joined_part.reshape(dp_count, group_rows, inputs),
            jnp.broadcast_to(gain_rows[None], (dp_count, 16, features)),
        ],
        axis=1,
    )
    joined_blocks = exchange(joined_part, dp_axes)
    gain_grad = joined_blocks[:, group_rows : group_rows + 3].astype(wide)
    gain_grad = ((gain_grad[:, 0] + gain_grad[:, 1]) + gain_grad[:, 2]).reshape(width)
    joined_total = jnp.sum(joined_blocks[:, :group_rows].astype(wide), axis=0).astype(narrow)
    joined_sent = other_first(joined_total.reshape(2, z_count, row_count, inputs))
    joined_grad = exchange(joined_sent.reshape(tensor_count, row_count, inputs), tensor_axes)
    joined_grad = joined_grad.transpose(1, 0, 2).reshape(row_count, tensor_count * inputs)

    kept_grad = token_sum(grad_half, mlp_all)
    other_grad = swap_cores(token_sum(grad_half, mlp_other))
    gate_weight_grad = jnp.where(on_first, kept_grad, other_grad)
    up_weight_grad = jnp.where(on_first, other_grad, kept_grad)
    joined_other = swap_cores(joined_half)
    join_kept = token_sum(joined_half, grad_all)
    join_other = token_sum(joined_other, grad_all)
    join_weight_grad = jnp.concatenate(
        [jnp.where(on_first, join_kept, join_other), jnp.where(on_first, join_other, join_kept)],
        axis=0,
    )
    return (joined_grad, gate_weight_grad, up_weight_grad, join_weight_grad, gain_grad)


def solution(mesh):
    tensor_count, dp_count = mesh.shape["tensor"], mesh.shape["dp"]
    fine = Mesh(
        mesh.devices.reshape(2, tensor_count // 2, dp_count // 4, 2, 2),
        ("y_lo", "z", "x", "y_hi", "core"),
    )
    tensor_axes = ("y_lo", "z")
    dp_axes = ("x", "y_hi", "core")
    rows = P(dp_axes + tensor_axes, None)
    blocks = P(tensor_axes, dp_axes)
    in_specs = (rows, rows, rows, rows, rows, rows, P(), blocks, blocks, blocks)
    out_specs = (rows, blocks, blocks, blocks, P())
    return jax.shard_map(shards, mesh=fine, in_specs=in_specs, out_specs=out_specs, check_vma=False)
```

```python
import jax
import jax.numpy as jnp
from jax import lax
from jax.sharding import Mesh
from jax.sharding import PartitionSpec as P

epsilon = 1e-05
narrow = jnp.bfloat16
wide = jnp.float32


def swiglu_back(gate_act, up_act, product_grad):
    gate_wide = gate_act.astype(wide)
    logistic = jax.nn.sigmoid(gate_wide)
    product_wide = product_grad.astype(wide)
    gate_grad = (
        product_wide * up_act.astype(wide) * logistic * (1.0 + gate_wide * (1.0 - logistic))
    )
    up_grad = product_wide * gate_wide * logistic
    return (gate_grad.astype(narrow), up_grad.astype(narrow))


def token_sum(left, right):
    return lax.dot_general(left, right, (((0,), (0,)), ((), ())), preferred_element_type=wide)


def exchange(blocks, axes):
    return lax.all_to_all(blocks, axes, split_axis=0, concat_axis=0, tiled=True)


def swap_cores(value):
    return lax.ppermute(value, "core", [(0, 1), (1, 0)])


def swap_near(value):
    return lax.ppermute(value, "y_lo", [(0, 1), (1, 0)])


def from_above(value, distance):
    count = lax.axis_size("z")
    return lax.ppermute(value, "z", [((i + distance) % count, i) for i in range(count)])


def gather_z(block):
    z_count = lax.axis_size("z")
    quarter = z_count // 4
    strided = jnp.stack([block] + [from_above(block, 4 * step) for step in range(1, quarter)])
    below = from_above(strided, z_count - 1)
    below = jnp.concatenate([below[1:], below[:1]])
    all_blocks = jnp.stack(
        [strided, from_above(strided, 1), from_above(strided, 2), below], axis=1
    ).reshape(z_count, *block.shape)
    twice = jnp.concatenate([all_blocks, all_blocks])
    return lax.dynamic_slice_in_dim(twice, z_count - lax.axis_index("z"), z_count, 0)


def trade_pair(blocks, axis_name):
    first = lax.axis_index(axis_name) == 0
    kept = jnp.where(first, blocks[0], blocks[1])
    sent = jnp.where(first, blocks[1], blocks[0])
    other = lax.ppermute(sent, axis_name, [(0, 1), (1, 0)])
    return jnp.stack([jnp.where(first, kept, other), jnp.where(first, other, kept)])


def trade_x(blocks):
    count, here = lax.axis_size("x"), lax.axis_index("x")
    turned = lax.dynamic_slice_in_dim(jnp.concatenate([blocks, blocks]), here, count, 0)
    pieces = [turned[0]] + [
        lax.ppermute(turned[step], "x", [(i, (i + step) % count) for i in range(count)])
        for step in range(1, count)
    ]
    back = jnp.stack([pieces[(count - step) % count] for step in range(count)])
    return lax.dynamic_slice_in_dim(jnp.concatenate([back, back]), count - here, count, 0)


def other_first(pair):
    return jnp.where(lax.axis_index("y_lo") == 0, pair[::-1], pair)


def split_three(value):
    high = value.astype(narrow)
    rest = value - high.astype(wide)
    middle = rest.astype(narrow)
    low = (rest - middle.astype(wide)).astype(narrow)
    return (high, middle, low)


def shards(
    hidden,
    joined_in,
    gate_act,
    up_act,
    product_grad,
    resid_grad,
    norm_gain,
    gate_weight,
    up_weight,
    join_weight,
):
    tensor_axes = ("y_lo", "z")
    dp_axes = ("x", "y_hi", "core")
    z_count = lax.axis_size("z")
    tensor_count = lax.axis_size("y_lo") * z_count
    core_count = lax.axis_size("core")
    dp_count = lax.axis_size("x") * lax.axis_size("y_hi") * core_count
    row_count, width = hidden.shape
    units, features = gate_weight.shape
    inputs = join_weight.shape[0]
    half_inputs = inputs // 2
    group_rows = tensor_count * row_count
    block_rows = dp_count * row_count
    tokens = dp_count * group_rows
    on_first = lax.axis_index("core") == 0

    weight_kept = jnp.where(on_first, gate_weight, up_weight)
    weight_other = swap_cores(jnp.where(on_first, up_weight, gate_weight))

    gate_grad, up_grad = swiglu_back(gate_act, up_act, product_grad)
    joined_rows = joined_in.reshape(row_count, tensor_count, 2, half_inputs)
    half_width = units + half_inputs
    gate_rows = jnp.concatenate(
        [gate_grad.reshape(row_count, tensor_count, units), joined_rows[:, :, 0]], axis=2
    )
    up_rows = jnp.concatenate(
        [up_grad.reshape(row_count, tensor_count, units), joined_rows[:, :, 1]], axis=2
    )
    unit_rows = jnp.stack([gate_rows, up_rows]).transpose(2, 0, 1, 3)
    unit_rows, hidden, resid_grad = lax.optimization_barrier((unit_rows, hidden, resid_grad))
    unit_group = exchange(
        unit_rows.reshape(tensor_count, 2 * row_count, half_width), tensor_axes
    )

    hidden_wide = hidden.astype(wide)
    row_scale = lax.rsqrt(jnp.mean(hidden_wide * hidden_wide, axis=1, keepdims=True) + epsilon)
    scale_parts = jnp.concatenate(split_three(row_scale), axis=1)
    scale_parts = jnp.pad(scale_parts, ((0, 0), (0, features - scale_parts.shape[1])))
    norm_rows = jnp.stack(
        [
            hidden.reshape(row_count, dp_count, features),
            resid_grad.reshape(row_count, dp_count, features),
            jnp.broadcast_to(scale_parts[:, None, :], (row_count, dp_count, features)),
        ]
    )
    norm_sent = norm_rows.transpose(2, 0, 1, 3).reshape(
        lax.axis_size("x"), 2, 2, 3 * row_count, features
    )
    norm_block = trade_pair(norm_sent.transpose(2, 0, 1, 3, 4), "core")
    norm_block = trade_pair(norm_block.transpose(2, 0, 1, 3, 4), "y_hi")
    norm_block = trade_x(norm_block.transpose(2, 0, 1, 3, 4)).reshape(
        dp_count, 3, row_count, features
    )
    hidden_block = norm_block[:, 0].reshape(block_rows, features).astype(wide)
    resid_block = norm_block[:, 1].reshape(block_rows, features).astype(wide)
    scale_block = norm_block[:, 2, :, :3].astype(wide).reshape(block_rows, 3)
    scale_block = (scale_block[:, 0:1] + scale_block[:, 1:2]) + scale_block[:, 2:3]
    gain_block = lax.dynamic_slice_in_dim(
        norm_gain, lax.axis_index(dp_axes) * features, features, 0
    )
    normed = hidden_block * scale_block
    mlp_block = (normed * gain_block).astype(narrow)

    unit_group, mlp_block = lax.optimization_barrier((unit_group, mlp_block))
    mlp_z = gather_z(mlp_block)
    unit_halves = (
        other_first(unit_group.reshape(2, z_count, 2, row_count, half_width))
        .transpose(2, 0, 1, 3, 4)
        .reshape(2, group_rows, half_width)
    )
    unit_halves = jnp.broadcast_to(
        unit_halves[None], (dp_count // core_count, core_count, group_rows, half_width)
    ).reshape(dp_count, group_rows, half_width)
    half_all = exchange(unit_halves, dp_axes).reshape(tokens, half_width)
    half_all, mlp_z = lax.optimization_barrier((half_all, mlp_z))
    mlp_all = (
        jnp.stack([swap_near(mlp_z), mlp_z])
        .reshape(2, z_count, dp_count, row_count, features)
        .transpose(2, 0, 1, 3, 4)
        .reshape(tokens, features)
    )
    mlp_other = swap_cores(mlp_all)
    grad_half = half_all[:, :units]
    joined_half = half_all[:, units:]

    sent_rows, kept_rows = (
        half_all.reshape(dp_count, 2, z_count * row_count, half_width)[:, side].reshape(
            -1, half_width
        )
        for side in range(2)
    )
    weight_other, weight_kept = (
        jnp.pad(weight, ((0, half_width - units), (0, 0)))
        for weight in (weight_other, weight_kept)
    )
    sent_other = swap_cores(jnp.dot(sent_rows, weight_other, preferred_element_type=wide))
    sent_own = jnp.dot(sent_rows, weight_kept, preferred_element_type=wide)
    near_part = swap_near((sent_own + sent_other).astype(narrow))
    kept_other = swap_cores(jnp.dot(kept_rows, weight_other, preferred_element_type=wide))
    kept_own = jnp.dot(kept_rows, weight_kept, preferred_element_type=wide)
    near_sum = kept_own + kept_other + near_part.astype(wide)
    near_sum = (
        near_sum.astype(narrow)
        .reshape(dp_count, z_count, row_count, features)
        .transpose(1, 0, 2, 3)
        .reshape(z_count, block_rows, features)
    )
    far = exchange(near_sum, "z")
    input_grad = jnp.sum(far.astype(wide), axis=0)

    lifted = input_grad * gain_block
    mean_part = jnp.sum(lifted * normed, axis=1)
    mean_all = exchange(
        jnp.broadcast_to(mean_part[None, None], (dp_count, 1, block_rows)), dp_axes
    )
    inner_mean = (jnp.sum(mean_all, axis=(0, 1)) / width)[:, None]
    hidden_grad = (resid_block + scale_block * (lifted - normed * inner_mean)).astype(narrow)
    gain_part = jnp.sum(input_grad * normed, axis=0, keepdims=True)

    grad_sent = jnp.concatenate(
        [hidden_grad] + list(split_three(gain_part)) + [jnp.zeros((5, features), narrow)], axis=0
    )
    grad_far = gather_z(grad_sent)
    grad_near = swap_near(grad_far)
    grad_pair = jnp.stack([grad_near, grad_far])
    gain_parts = other_first(grad_pair[:, :, block_rows : block_rows + 3]).astype(wide)
    gain_sum = jnp.sum(gain_parts, axis=(0, 1, 2))[None]
    grad_all = (
        grad_pair[:, :, :block_rows]
        .reshape(tensor_count, dp_count, row_count, features)
        .transpose(1, 0, 2, 3)
        .reshape(tokens, features)
    )
    joined_part = lax.dot_general(
        grad_all, join_weight, (((1,), (1,)), ((), ())), preferred_element_type=wide
    ).astype(narrow)
    gain_rows = jnp.concatenate(
        list(split_three(gain_sum)) + [jnp.zeros((13, features), narrow)], axis=0
    )
    joined_part = jnp.concatenate(
        [
            joined_part.reshape(dp_count, group_rows, inputs),
            jnp.broadcast_to(gain_rows[None], (dp_count, 16, features)),
        ],
        axis=1,
    )
    joined_blocks = exchange(joined_part, dp_axes)
    gain_grad = joined_blocks[:, group_rows : group_rows + 3].astype(wide)
    gain_grad = ((gain_grad[:, 0] + gain_grad[:, 1]) + gain_grad[:, 2]).reshape(width)
    joined_total = jnp.sum(joined_blocks[:, :group_rows].astype(wide), axis=0).astype(narrow)
    joined_sent = other_first(joined_total.reshape(2, z_count, row_count, inputs))
    joined_grad = exchange(joined_sent.reshape(tensor_count, row_count, inputs), tensor_axes)
    joined_grad = joined_grad.transpose(1, 0, 2).reshape(row_count, tensor_count * inputs)

    kept_grad = token_sum(grad_half, mlp_all)
    other_grad = swap_cores(token_sum(grad_half, mlp_other))
    gate_weight_grad = jnp.where(on_first, kept_grad, other_grad)
    up_weight_grad = jnp.where(on_first, other_grad, kept_grad)
    joined_other = swap_cores(joined_half)
    join_kept = token_sum(joined_half, grad_all)
    join_other = token_sum(joined_other, grad_all)
    join_weight_grad = jnp.concatenate(
        [jnp.where(on_first, join_kept, join_other), jnp.where(on_first, join_other, join_kept)],
        axis=0,
    )
    return (joined_grad, gate_weight_grad, up_weight_grad, join_weight_grad, gain_grad)


def solution(mesh):
    tensor_count, dp_count = mesh.shape["tensor"], mesh.shape["dp"]
    fine = Mesh(
        mesh.devices.reshape(2, tensor_count // 2, dp_count // 4, 2, 2),
        ("y_lo", "z", "x", "y_hi", "core"),
    )
    tensor_axes = ("y_lo", "z")
    dp_axes = ("x", "y_hi", "core")
    rows = P(dp_axes + tensor_axes, None)
    blocks = P(tensor_axes, dp_axes)
    in_specs = (rows, rows, rows, rows, rows, rows, P(), blocks, blocks, blocks)
    out_specs = (rows, blocks, blocks, blocks, P())
    return jax.shard_map(shards, mesh=fine, in_specs=in_specs, out_specs=out_specs, check_vma=False)
```

```python
import jax
import jax.numpy as jnp
from jax import lax
from jax.sharding import Mesh
from jax.sharding import PartitionSpec as P

epsilon = 1e-05
narrow = jnp.bfloat16
wide = jnp.float32


def swiglu_back(gate_act, up_act, product_grad):
    gate_wide = gate_act.astype(wide)
    logistic = jax.nn.sigmoid(gate_wide)
    product_wide = product_grad.astype(wide)
    gate_grad = (
        product_wide * up_act.astype(wide) * logistic * (1.0 + gate_wide * (1.0 - logistic))
    )
    up_grad = product_wide * gate_wide * logistic
    return (gate_grad.astype(narrow), up_grad.astype(narrow))


def token_sum(left, right):
    return lax.dot_general(left, right, (((0,), (0,)), ((), ())), preferred_element_type=wide)


def exchange(blocks, axes):
    return lax.all_to_all(blocks, axes, split_axis=0, concat_axis=0, tiled=True)


def swap_cores(value):
    return lax.ppermute(value, "core", [(0, 1), (1, 0)])


def swap_near(value):
    return lax.ppermute(value, "y_lo", [(0, 1), (1, 0)])


def from_above(value, distance):
    count = lax.axis_size("z")
    return lax.ppermute(value, "z", [((i + distance) % count, i) for i in range(count)])


def gather_z(block):
    z_count = lax.axis_size("z")
    quarter = z_count // 4
    strided = jnp.stack([block] + [from_above(block, 4 * step) for step in range(1, quarter)])
    below = from_above(strided, z_count - 1)
    below = jnp.concatenate([below[1:], below[:1]])
    all_blocks = jnp.stack(
        [strided, from_above(strided, 1), from_above(strided, 2), below], axis=1
    ).reshape(z_count, *block.shape)
    twice = jnp.concatenate([all_blocks, all_blocks])
    return lax.dynamic_slice_in_dim(twice, z_count - lax.axis_index("z"), z_count, 0)


def trade_pair(blocks, axis_name):
    first = lax.axis_index(axis_name) == 0
    kept = jnp.where(first, blocks[0], blocks[1])
    sent = jnp.where(first, blocks[1], blocks[0])
    other = lax.ppermute(sent, axis_name, [(0, 1), (1, 0)])
    return jnp.stack([jnp.where(first, kept, other), jnp.where(first, other, kept)])


def trade_x(blocks):
    count, here = lax.axis_size("x"), lax.axis_index("x")
    turned = lax.dynamic_slice_in_dim(jnp.concatenate([blocks, blocks]), here, count, 0)
    pieces = [turned[0]] + [
        lax.ppermute(turned[step], "x", [(i, (i + step) % count) for i in range(count)])
        for step in range(1, count)
    ]
    back = jnp.stack([pieces[(count - step) % count] for step in range(count)])
    return lax.dynamic_slice_in_dim(jnp.concatenate([back, back]), count - here, count, 0)


def split_three(value):
    high = value.astype(narrow)
    rest = value - high.astype(wide)
    middle = rest.astype(narrow)
    low = (rest - middle.astype(wide)).astype(narrow)
    return (high, middle, low)


def shards(
    hidden,
    joined_in,
    gate_act,
    up_act,
    product_grad,
    resid_grad,
    norm_gain,
    gate_weight,
    up_weight,
    join_weight,
):
    dp_axes = ("x", "y_hi", "core")
    z_count = lax.axis_size("z")
    core_count = lax.axis_size("core")
    dp_count = lax.axis_size("x") * lax.axis_size("y_hi") * core_count
    row_count, width = hidden.shape
    units, features = gate_weight.shape
    inputs = join_weight.shape[0]
    half_inputs = inputs // 2
    part_width = units + half_inputs
    plane_rows = z_count * row_count
    block_rows = dp_count * row_count
    tokens = dp_count * plane_rows
    on_first = lax.axis_index("core") == 0
    here = lax.axis_index("y_lo")
    near_first = here == 0

    def by_near(own, near):
        return jnp.stack([jnp.where(near_first, own, near), jnp.where(near_first, near, own)])

    def by_core(own, other):
        return jnp.stack([jnp.where(on_first, own, other), jnp.where(on_first, other, own)])

    gate_grad, up_grad = swiglu_back(gate_act, up_act, product_grad)
    joined_rows = joined_in.reshape(row_count, 2, z_count, 2, half_inputs)
    gate_rows = jnp.concatenate(
        [gate_grad.reshape(row_count, 2, z_count, units), joined_rows[:, :, :, 0]], axis=3
    )
    up_rows = jnp.concatenate(
        [up_grad.reshape(row_count, 2, z_count, units), joined_rows[:, :, :, 1]], axis=3
    )
    unit_rows = jnp.stack([gate_rows, up_rows]).transpose(3, 0, 1, 2, 4)
    unit_rows = unit_rows.reshape(z_count, 2 * row_count, 2 * part_width)
    unit_rows, hidden, resid_grad = lax.optimization_barrier((unit_rows, hidden, resid_grad))
    unit_group = exchange(unit_rows, "z")

    weight_own = jnp.where(on_first, gate_weight, up_weight)
    weight_other = swap_cores(jnp.where(on_first, up_weight, gate_weight))
    near_own, near_other = swap_near(weight_own), swap_near(weight_other)
    near_join = swap_near(join_weight)

    hidden_wide = hidden.astype(wide)
    row_scale = lax.rsqrt(jnp.mean(hidden_wide * hidden_wide, axis=1, keepdims=True) + epsilon)
    scale_parts = jnp.concatenate(split_three(row_scale), axis=1)
    scale_parts = jnp.pad(scale_parts, ((0, 0), (0, features - scale_parts.shape[1])))
    norm_rows = jnp.stack(
        [
            hidden.reshape(row_count, dp_count, features),
            resid_grad.reshape(row_count, dp_count, features),
            jnp.broadcast_to(scale_parts[:, None, :], (row_count, dp_count, features)),
        ]
    )
    norm_sent = norm_rows.transpose(2, 0, 1, 3).reshape(
        lax.axis_size("x"), 2, 2, 3 * row_count, features
    )
    norm_block = trade_pair(norm_sent.transpose(2, 0, 1, 3, 4), "core")
    norm_block = trade_pair(norm_block.transpose(2, 0, 1, 3, 4), "y_hi")
    norm_block = trade_x(norm_block.transpose(2, 0, 1, 3, 4)).reshape(
        dp_count, 3, row_count, features
    )
    hidden_block = norm_block[:, 0].reshape(block_rows, features).astype(wide)
    resid_block = norm_block[:, 1].reshape(block_rows, features).astype(wide)
    scale_block = norm_block[:, 2, :, :3].astype(wide).reshape(block_rows, 3)
    scale_block = (scale_block[:, 0:1] + scale_block[:, 1:2]) + scale_block[:, 2:3]
    gain_block = lax.dynamic_slice_in_dim(
        norm_gain, lax.axis_index(dp_axes) * features, features, 0
    )
    normed = hidden_block * scale_block
    mlp_block = (normed * gain_block).astype(narrow)

    unit_group, mlp_block, near_own, near_other = lax.optimization_barrier(
        (unit_group, mlp_block, near_own, near_other)
    )
    mlp_z = gather_z(mlp_block)
    unit_halves = (
        unit_group.reshape(z_count, 2, row_count, 2 * part_width)
        .transpose(1, 0, 2, 3)
        .reshape(2, plane_rows, 2 * part_width)
    )
    unit_halves = jnp.broadcast_to(
        unit_halves[None], (dp_count // core_count, core_count, plane_rows, 2 * part_width)
    ).reshape(dp_count, plane_rows, 2 * part_width)
    half_all = exchange(unit_halves, dp_axes).reshape(tokens, 2 * part_width)
    half_all, mlp_z = lax.optimization_barrier((half_all, mlp_z))

    def both_near(own, near):
        both = jnp.pad(by_near(own, near), ((0, 0), (0, half_inputs), (0, 0)))
        return both.reshape(2 * part_width, features)

    partial_other = jnp.dot(
        half_all, both_near(weight_other, near_other), preferred_element_type=wide
    )
    partial_own = jnp.dot(half_all, both_near(weight_own, near_own), preferred_element_type=wide)
    partial_value = partial_own + swap_cores(partial_other)
    partial_value = (
        partial_value.astype(narrow)
        .reshape(dp_count, z_count, row_count, features)
        .transpose(1, 0, 2, 3)
        .reshape(z_count, block_rows, features)
    )
    input_grad = jnp.sum(exchange(partial_value, "z").astype(wide), axis=0)

    lifted = input_grad * gain_block
    mean_part = jnp.sum(lifted * normed, axis=1)
    mean_all = exchange(
        jnp.broadcast_to(mean_part[None, None], (dp_count, 1, block_rows)), dp_axes
    )
    inner_mean = (jnp.sum(mean_all, axis=(0, 1)) / width)[:, None]
    hidden_grad = (resid_block + scale_block * (lifted - normed * inner_mean)).astype(narrow)
    gain_part = jnp.sum(input_grad * normed, axis=0, keepdims=True)

    sent_rows = block_rows + 8
    grad_sent = jnp.concatenate(
        [hidden_grad] + list(split_three(gain_part)) + [jnp.zeros((5, features), narrow)], axis=0
    )
    grad_z = exchange(jnp.broadcast_to(grad_sent[None], (z_count, sent_rows, features)), "z")
    gain_sum = jnp.sum(grad_z[:, block_rows : block_rows + 3].astype(wide), axis=(0, 1))[None]
    grad_all = (
        grad_z[:, :block_rows]
        .reshape(z_count, dp_count, row_count, features)
        .transpose(1, 0, 2, 3)
        .reshape(tokens, features)
    )

    join_both = by_near(join_weight, near_join).reshape(2 * inputs, features)
    joined_part = lax.dot_general(
        grad_all, join_both, (((1,), (1,)), ((), ())), preferred_element_type=wide
    ).astype(narrow)
    gain_rows = jnp.concatenate(
        list(split_three(gain_sum)) + [jnp.zeros((13, features), narrow)], axis=0
    ).reshape(8, 2 * features)
    joined_part = jnp.concatenate(
        [
            joined_part.reshape(dp_count, plane_rows, 2 * inputs),
            jnp.broadcast_to(gain_rows[None], (dp_count, 8, 2 * features)),
        ],
        axis=1,
    )
    joined_blocks = exchange(joined_part, dp_axes)
    gain_blocks = joined_blocks[:, plane_rows : plane_rows + 2].astype(wide)
    gain_own = (gain_blocks[:, 0, :features] + gain_blocks[:, 0, features:]) + gain_blocks[
        :, 1, :features
    ]
    gain_grad = (gain_own + swap_near(gain_own)).reshape(width)
    joined_total = jnp.sum(joined_blocks[:, :plane_rows].astype(wide), axis=0).astype(narrow)
    joined_grad = exchange(joined_total.reshape(z_count, row_count, 2 * inputs), "z")
    joined_grad = (
        joined_grad.reshape(z_count, row_count, 2, inputs)
        .transpose(1, 2, 0, 3)
        .reshape(row_count, 2 * z_count * inputs)
    )

    mlp_own = (
        mlp_z.reshape(z_count, dp_count, row_count, features)
        .transpose(1, 0, 2, 3)
        .reshape(tokens, features)
    )

    def add_near(sums):
        kept = lax.dynamic_index_in_dim(sums, here, 0, keepdims=False)
        sent = lax.dynamic_index_in_dim(sums, 1 - here, 0, keepdims=False)
        return kept + swap_near(sent)

    def unit_sums(mlp_input):
        sums = token_sum(half_all, mlp_input).reshape(2, part_width, features)
        return add_near(sums[:, :units])

    other_grad = swap_cores(unit_sums(swap_cores(mlp_own)))
    own_grad = unit_sums(mlp_own)
    gate_weight_grad = jnp.where(on_first, own_grad, other_grad)
    up_weight_grad = jnp.where(on_first, other_grad, own_grad)

    joined_half = jnp.concatenate(
        [half_all[:, units:part_width], half_all[:, part_width + units :]], axis=1
    )
    join_sums = by_core(
        token_sum(joined_half, grad_all).reshape(2, half_inputs, features),
        token_sum(swap_cores(joined_half), grad_all).reshape(2, half_inputs, features),
    )
    join_weight_grad = add_near(join_sums.transpose(1, 0, 2, 3)).reshape(inputs, features)
    return (joined_grad, gate_weight_grad, up_weight_grad, join_weight_grad, gain_grad)


def solution(mesh):
    tensor_count, dp_count = mesh.shape["tensor"], mesh.shape["dp"]
    fine = Mesh(
        mesh.devices.reshape(2, tensor_count // 2, dp_count // 4, 2, 2),
        ("y_lo", "z", "x", "y_hi", "core"),
    )
    tensor_axes = ("y_lo", "z")
    dp_axes = ("x", "y_hi", "core")
    rows = P(dp_axes + tensor_axes, None)
    blocks = P(tensor_axes, dp_axes)
    in_specs = (rows, rows, rows, rows, rows, rows, P(), blocks, blocks, blocks)
    out_specs = (rows, blocks, blocks, blocks, P())
    return jax.shard_map(shards, mesh=fine, in_specs=in_specs, out_specs=out_specs, check_vma=False)
```

```python
import jax
import jax.numpy as jnp
from jax import lax
from jax.sharding import Mesh
from jax.sharding import PartitionSpec as P

epsilon = 1e-05
narrow = jnp.bfloat16
wide = jnp.float32


def swiglu_back(gate_act, up_act, product_grad):
    gate_wide = gate_act.astype(wide)
    logistic = jax.nn.sigmoid(gate_wide)
    product_wide = product_grad.astype(wide)
    gate_grad = (
        product_wide * up_act.astype(wide) * logistic * (1.0 + gate_wide * (1.0 - logistic))
    )
    up_grad = product_wide * gate_wide * logistic
    return (gate_grad.astype(narrow), up_grad.astype(narrow))


def token_sum(left, right):
    return lax.dot_general(left, right, (((0,), (0,)), ((), ())), preferred_element_type=wide)


def exchange(blocks, axes):
    return lax.all_to_all(blocks, axes, split_axis=0, concat_axis=0, tiled=True)


def swap_cores(value):
    return lax.ppermute(value, "core", [(0, 1), (1, 0)])


def swap_near(value):
    return lax.ppermute(value, "y_lo", [(0, 1), (1, 0)])


def from_above(value, distance):
    count = lax.axis_size("z")
    return lax.ppermute(value, "z", [((i + distance) % count, i) for i in range(count)])


def gather_z(block):
    z_count = lax.axis_size("z")
    quarter = z_count // 4
    strided = jnp.stack([block] + [from_above(block, 4 * step) for step in range(1, quarter)])
    below = from_above(strided, z_count - 1)
    below = jnp.concatenate([below[1:], below[:1]])
    all_blocks = jnp.stack(
        [strided, from_above(strided, 1), from_above(strided, 2), below], axis=1
    ).reshape(z_count, *block.shape)
    twice = jnp.concatenate([all_blocks, all_blocks])
    return lax.dynamic_slice_in_dim(twice, z_count - lax.axis_index("z"), z_count, 0)


def trade_pair(blocks, axis_name):
    first = lax.axis_index(axis_name) == 0
    kept = jnp.where(first, blocks[0], blocks[1])
    sent = jnp.where(first, blocks[1], blocks[0])
    other = lax.ppermute(sent, axis_name, [(0, 1), (1, 0)])
    return jnp.stack([jnp.where(first, kept, other), jnp.where(first, other, kept)])


def trade_x(blocks):
    count, here = lax.axis_size("x"), lax.axis_index("x")
    turned = lax.dynamic_slice_in_dim(jnp.concatenate([blocks, blocks]), here, count, 0)
    pieces = [turned[0]] + [
        lax.ppermute(turned[step], "x", [(i, (i + step) % count) for i in range(count)])
        for step in range(1, count)
    ]
    back = jnp.stack([pieces[(count - step) % count] for step in range(count)])
    return lax.dynamic_slice_in_dim(jnp.concatenate([back, back]), count - here, count, 0)


def split_three(value):
    high = value.astype(narrow)
    rest = value - high.astype(wide)
    middle = rest.astype(narrow)
    low = (rest - middle.astype(wide)).astype(narrow)
    return (high, middle, low)


def shards(
    hidden,
    joined_in,
    gate_act,
    up_act,
    product_grad,
    resid_grad,
    norm_gain,
    gate_weight,
    up_weight,
    join_weight,
):
    dp_axes = ("x", "y_hi", "core")
    z_count = lax.axis_size("z")
    core_count = lax.axis_size("core")
    dp_count = lax.axis_size("x") * lax.axis_size("y_hi") * core_count
    row_count, width = hidden.shape
    units, features = gate_weight.shape
    inputs = join_weight.shape[0]
    half_inputs = inputs // 2
    part_width = units + half_inputs
    plane_rows = z_count * row_count
    block_rows = dp_count * row_count
    tokens = dp_count * plane_rows
    on_first = lax.axis_index("core") == 0
    here = lax.axis_index("y_lo")
    near_first = here == 0

    def by_near(own, near):
        return jnp.stack([jnp.where(near_first, own, near), jnp.where(near_first, near, own)])

    def by_core(own, other):
        return jnp.stack([jnp.where(on_first, own, other), jnp.where(on_first, other, own)])

    gate_grad, up_grad = swiglu_back(gate_act, up_act, product_grad)
    joined_rows = joined_in.reshape(row_count, 2, z_count, 2, half_inputs)
    gate_rows = jnp.concatenate(
        [gate_grad.reshape(row_count, 2, z_count, units), joined_rows[:, :, :, 0]], axis=3
    )
    up_rows = jnp.concatenate(
        [up_grad.reshape(row_count, 2, z_count, units), joined_rows[:, :, :, 1]], axis=3
    )
    unit_rows = jnp.stack([gate_rows, up_rows]).transpose(3, 0, 1, 2, 4)
    unit_rows = unit_rows.reshape(z_count, 2 * row_count, 2 * part_width)
    unit_rows, hidden, resid_grad = lax.optimization_barrier((unit_rows, hidden, resid_grad))
    unit_group = exchange(unit_rows, "z")

    weight_own = jnp.where(on_first, gate_weight, up_weight)
    weight_other = swap_cores(jnp.where(on_first, up_weight, gate_weight))
    near_join = swap_near(join_weight)

    hidden_wide = hidden.astype(wide)
    row_scale = lax.rsqrt(jnp.mean(hidden_wide * hidden_wide, axis=1, keepdims=True) + epsilon)
    scale_parts = jnp.concatenate(split_three(row_scale), axis=1)
    scale_parts = jnp.pad(scale_parts, ((0, 0), (0, features - scale_parts.shape[1])))
    norm_rows = jnp.stack(
        [
            hidden.reshape(row_count, dp_count, features),
            resid_grad.reshape(row_count, dp_count, features),
            jnp.broadcast_to(scale_parts[:, None, :], (row_count, dp_count, features)),
        ]
    )
    norm_sent = norm_rows.transpose(2, 0, 1, 3).reshape(
        lax.axis_size("x"), 2, 2, 3 * row_count, features
    )
    norm_block = trade_pair(norm_sent.transpose(2, 0, 1, 3, 4), "core")
    norm_block, near_own = lax.optimization_barrier((norm_block, swap_near(weight_own)))
    norm_block = trade_pair(norm_block.transpose(2, 0, 1, 3, 4), "y_hi")
    norm_block, weight_other = lax.optimization_barrier((norm_block, weight_other))
    near_other = swap_near(weight_other)
    norm_block = trade_x(norm_block.transpose(2, 0, 1, 3, 4)).reshape(
        dp_count, 3, row_count, features
    )
    hidden_block = norm_block[:, 0].reshape(block_rows, features).astype(wide)
    resid_block = norm_block[:, 1].reshape(block_rows, features).astype(wide)
    scale_block = norm_block[:, 2, :, :3].astype(wide).reshape(block_rows, 3)
    scale_block = (scale_block[:, 0:1] + scale_block[:, 1:2]) + scale_block[:, 2:3]
    gain_block = lax.dynamic_slice_in_dim(
        norm_gain, lax.axis_index(dp_axes) * features, features, 0
    )
    normed = hidden_block * scale_block
    mlp_block = (normed * gain_block).astype(narrow)

    unit_group, mlp_block, near_other = lax.optimization_barrier(
        (unit_group, mlp_block, near_other)
    )
    mlp_z = gather_z(mlp_block)
    unit_halves = (
        unit_group.reshape(z_count, 2, row_count, 2 * part_width)
        .transpose(1, 0, 2, 3)
        .reshape(2, plane_rows, 2 * part_width)
    )
    unit_halves = jnp.broadcast_to(
        unit_halves[None], (dp_count // core_count, core_count, plane_rows, 2 * part_width)
    ).reshape(dp_count, plane_rows, 2 * part_width)
    half_all = exchange(unit_halves, dp_axes).reshape(tokens, 2 * part_width)
    half_all, mlp_z = lax.optimization_barrier((half_all, mlp_z))

    def both_near(own, near):
        both = jnp.pad(by_near(own, near), ((0, 0), (0, half_inputs), (0, 0)))
        return both.reshape(2 * part_width, features)

    partial_other = jnp.dot(
        half_all, both_near(weight_other, near_other), preferred_element_type=wide
    )
    partial_own = jnp.dot(half_all, both_near(weight_own, near_own), preferred_element_type=wide)
    partial_value = partial_own + swap_cores(partial_other)
    partial_value = (
        partial_value.astype(narrow)
        .reshape(dp_count, z_count, row_count, features)
        .transpose(1, 0, 2, 3)
        .reshape(z_count, block_rows, features)
    )

    mlp_own = (
        mlp_z.reshape(z_count, dp_count, row_count, features)
        .transpose(1, 0, 2, 3)
        .reshape(tokens, features)
    )
    unit_sums = token_sum(half_all, jnp.concatenate([mlp_own, swap_cores(mlp_own)], axis=1))
    partial_far, unit_sums = lax.optimization_barrier((exchange(partial_value, "z"), unit_sums))
    unit_sums = unit_sums.reshape(2, part_width, 2 * features)[:, :units]
    unit_kept = lax.dynamic_index_in_dim(unit_sums, here, 0, keepdims=False)
    unit_near = swap_near(
        lax.dynamic_index_in_dim(unit_sums, 1 - here, 0, keepdims=False).astype(narrow)
    )
    input_grad = jnp.sum(partial_far.astype(wide), axis=0)

    lifted = input_grad * gain_block
    mean_part = jnp.sum(lifted * normed, axis=1)
    mean_all = exchange(
        jnp.broadcast_to(mean_part[None, None], (dp_count, 1, block_rows)), dp_axes
    )
    inner_mean = (jnp.sum(mean_all, axis=(0, 1)) / width)[:, None]
    hidden_grad = (resid_block + scale_block * (lifted - normed * inner_mean)).astype(narrow)
    gain_part = jnp.sum(input_grad * normed, axis=0, keepdims=True)

    sent_rows = block_rows + 8
    grad_sent = jnp.concatenate(
        [hidden_grad] + list(split_three(gain_part)) + [jnp.zeros((5, features), narrow)], axis=0
    )
    grad_z = exchange(jnp.broadcast_to(grad_sent[None], (z_count, sent_rows, features)), "z")
    grad_z, unit_near = lax.optimization_barrier((grad_z, unit_near))
    gain_sum = jnp.sum(grad_z[:, block_rows : block_rows + 3].astype(wide), axis=(0, 1))[None]
    grad_all = (
        grad_z[:, :block_rows]
        .reshape(z_count, dp_count, row_count, features)
        .transpose(1, 0, 2, 3)
        .reshape(tokens, features)
    )

    join_both = by_near(join_weight, near_join).reshape(2 * inputs, features)
    joined_part = lax.dot_general(
        grad_all, join_both, (((1,), (1,)), ((), ())), preferred_element_type=wide
    ).astype(narrow)
    gain_rows = jnp.concatenate(
        list(split_three(gain_sum)) + [jnp.zeros((13, features), narrow)], axis=0
    ).reshape(8, 2 * features)
    joined_part = jnp.concatenate(
        [
            joined_part.reshape(dp_count, plane_rows, 2 * inputs),
            jnp.broadcast_to(gain_rows[None], (dp_count, 8, 2 * features)),
        ],
        axis=1,
    )
    joined_blocks = exchange(joined_part, dp_axes)
    gain_blocks = joined_blocks[:, plane_rows : plane_rows + 2].astype(wide)
    gain_own = (gain_blocks[:, 0, :features] + gain_blocks[:, 0, features:]) + gain_blocks[
        :, 1, :features
    ]
    gain_grad = (gain_own + swap_near(gain_own)).reshape(width)
    joined_total = jnp.sum(joined_blocks[:, :plane_rows].astype(wide), axis=0).astype(narrow)
    joined_grad = exchange(joined_total.reshape(z_count, row_count, 2 * inputs), "z")
    joined_grad = (
        joined_grad.reshape(z_count, row_count, 2, inputs)
        .transpose(1, 2, 0, 3)
        .reshape(row_count, 2 * z_count * inputs)
    )

    unit_grad = unit_kept + unit_near.astype(wide)
    own_grad = unit_grad[:, :features]
    other_grad = swap_cores(unit_grad[:, features:])
    gate_weight_grad = jnp.where(on_first, own_grad, other_grad)
    up_weight_grad = jnp.where(on_first, other_grad, own_grad)

    def add_near(sums):
        kept = lax.dynamic_index_in_dim(sums, here, 0, keepdims=False)
        sent = lax.dynamic_index_in_dim(sums, 1 - here, 0, keepdims=False)
        return kept + swap_near(sent)

    joined_half = jnp.concatenate(
        [half_all[:, units:part_width], half_all[:, part_width + units :]], axis=1
    )
    join_sums = by_core(
        token_sum(joined_half, grad_all).reshape(2, half_inputs, features),
        token_sum(swap_cores(joined_half), grad_all).reshape(2, half_inputs, features),
    )
    join_weight_grad = add_near(join_sums.transpose(1, 0, 2, 3)).reshape(inputs, features)
    return (joined_grad, gate_weight_grad, up_weight_grad, join_weight_grad, gain_grad)


def solution(mesh):
    tensor_count, dp_count = mesh.shape["tensor"], mesh.shape["dp"]
    fine = Mesh(
        mesh.devices.reshape(2, tensor_count // 2, dp_count // 4, 2, 2),
        ("y_lo", "z", "x", "y_hi", "core"),
    )
    tensor_axes = ("y_lo", "z")
    dp_axes = ("x", "y_hi", "core")
    rows = P(dp_axes + tensor_axes, None)
    blocks = P(tensor_axes, dp_axes)
    in_specs = (rows, rows, rows, rows, rows, rows, P(), blocks, blocks, blocks)
    out_specs = (rows, blocks, blocks, blocks, P())
    return jax.shard_map(shards, mesh=fine, in_specs=in_specs, out_specs=out_specs, check_vma=False)
```

```python
import jax
import jax.numpy as jnp
from jax import lax
from jax.sharding import Mesh
from jax.sharding import PartitionSpec as P

epsilon = 1e-05
narrow = jnp.bfloat16
wide = jnp.float32


def swiglu_back(gate_act, up_act, product_grad):
    gate_wide = gate_act.astype(wide)
    logistic = jax.nn.sigmoid(gate_wide)
    product_wide = product_grad.astype(wide)
    gate_grad = (
        product_wide * up_act.astype(wide) * logistic * (1.0 + gate_wide * (1.0 - logistic))
    )
    up_grad = product_wide * gate_wide * logistic
    return (gate_grad.astype(narrow), up_grad.astype(narrow))


def token_sum(left, right):
    return lax.dot_general(left, right, (((0,), (0,)), ((), ())), preferred_element_type=wide)


def exchange(blocks, axes):
    return lax.all_to_all(blocks, axes, split_axis=0, concat_axis=0, tiled=True)


def swap_cores(value):
    return lax.ppermute(value, "core", [(0, 1), (1, 0)])


def swap_near(value):
    return lax.ppermute(value, "y_lo", [(0, 1), (1, 0)])


def from_above(value, distance):
    count = lax.axis_size("z")
    return lax.ppermute(value, "z", [((i + distance) % count, i) for i in range(count)])


def gather_z(block):
    z_count = lax.axis_size("z")
    quarter = z_count // 4
    strided = jnp.stack([block] + [from_above(block, 4 * step) for step in range(1, quarter)])
    below = from_above(strided, z_count - 1)
    below = jnp.concatenate([below[1:], below[:1]])
    all_blocks = jnp.stack(
        [strided, from_above(strided, 1), from_above(strided, 2), below], axis=1
    ).reshape(z_count, *block.shape)
    return from_first(all_blocks)


def gather_z_relay(block):
    z_count = lax.axis_size("z")
    half = block.shape[0] // 2
    above, below = from_above(block, 4), from_above(block, z_count - 4)
    far = jnp.concatenate(
        [from_above(above[:half], 4), from_above(below[half:], z_count - 4)]
    )
    strided = jnp.stack([block, above, far, below])
    above, below = from_above(strided, 1), from_above(strided, z_count - 1)
    far = jnp.concatenate(
        [
            from_above(above[:2], 1),
            from_above(jnp.concatenate([below[3:], below[:1]]), z_count - 1),
        ]
    )
    below = jnp.concatenate([below[1:], below[:1]])
    return jnp.stack([strided, above, far, below], axis=1).reshape(z_count, *block.shape)


def from_first(blocks):
    twice = jnp.concatenate([blocks, blocks])
    count = blocks.shape[0]
    return lax.dynamic_slice_in_dim(twice, count - lax.axis_index("z"), count, 0)


def trade_pair(blocks, axis_name):
    first = lax.axis_index(axis_name) == 0
    kept = jnp.where(first, blocks[0], blocks[1])
    sent = jnp.where(first, blocks[1], blocks[0])
    other = lax.ppermute(sent, axis_name, [(0, 1), (1, 0)])
    return jnp.stack([jnp.where(first, kept, other), jnp.where(first, other, kept)])


def trade_x(blocks):
    count, here = lax.axis_size("x"), lax.axis_index("x")
    turned = lax.dynamic_slice_in_dim(jnp.concatenate([blocks, blocks]), here, count, 0)
    pieces = [turned[0]] + [
        lax.ppermute(turned[step], "x", [(i, (i + step) % count) for i in range(count)])
        for step in range(1, count)
    ]
    back = jnp.stack([pieces[(count - step) % count] for step in range(count)])
    return lax.dynamic_slice_in_dim(jnp.concatenate([back, back]), count - here, count, 0)


def split_three(value):
    high = value.astype(narrow)
    rest = value - high.astype(wide)
    middle = rest.astype(narrow)
    low = (rest - middle.astype(wide)).astype(narrow)
    return (high, middle, low)


def shards(
    hidden,
    joined_in,
    gate_act,
    up_act,
    product_grad,
    resid_grad,
    norm_gain,
    gate_weight,
    up_weight,
    join_weight,
):
    dp_axes = ("x", "y_hi", "core")
    z_count = lax.axis_size("z")
    core_count = lax.axis_size("core")
    dp_count = lax.axis_size("x") * lax.axis_size("y_hi") * core_count
    row_count, width = hidden.shape
    units, features = gate_weight.shape
    inputs = join_weight.shape[0]
    half_inputs = inputs // 2
    part_width = units + half_inputs
    plane_rows = z_count * row_count
    block_rows = dp_count * row_count
    tokens = dp_count * plane_rows
    on_first = lax.axis_index("core") == 0
    here = lax.axis_index("y_lo")
    near_first = here == 0

    def by_near(own, near):
        return jnp.stack([jnp.where(near_first, own, near), jnp.where(near_first, near, own)])

    def by_core(own, other):
        return jnp.stack([jnp.where(on_first, own, other), jnp.where(on_first, other, own)])

    gate_grad, up_grad = swiglu_back(gate_act, up_act, product_grad)
    joined_rows = joined_in.reshape(row_count, 2, z_count, 2, half_inputs)
    gate_rows = jnp.concatenate(
        [gate_grad.reshape(row_count, 2, z_count, units), joined_rows[:, :, :, 0]], axis=3
    )
    up_rows = jnp.concatenate(
        [up_grad.reshape(row_count, 2, z_count, units), joined_rows[:, :, :, 1]], axis=3
    )
    unit_rows = jnp.stack([gate_rows, up_rows]).transpose(3, 0, 1, 2, 4)
    unit_rows = unit_rows.reshape(z_count, 2 * row_count, 2 * part_width)
    unit_rows, hidden, resid_grad = lax.optimization_barrier((unit_rows, hidden, resid_grad))
    unit_group = exchange(unit_rows, "z")

    hidden_wide = hidden.astype(wide)
    row_scale = lax.rsqrt(jnp.mean(hidden_wide * hidden_wide, axis=1, keepdims=True) + epsilon)
    scale_parts = jnp.concatenate(split_three(row_scale), axis=1)
    scale_parts = jnp.pad(scale_parts, ((0, 0), (0, features - scale_parts.shape[1])))
    norm_rows = jnp.stack(
        [
            hidden.reshape(row_count, dp_count, features),
            resid_grad.reshape(row_count, dp_count, features),
            jnp.broadcast_to(scale_parts[:, None, :], (row_count, dp_count, features)),
        ]
    )
    norm_sent = norm_rows.transpose(2, 0, 1, 3).reshape(
        lax.axis_size("x"), 2, 2, 3 * row_count, features
    )
    norm_block = trade_pair(norm_sent.transpose(2, 0, 1, 3, 4), "core")
    norm_block, near_gate, near_up = lax.optimization_barrier(
        (norm_block, swap_near(gate_weight), swap_near(up_weight))
    )
    norm_block = trade_pair(norm_block.transpose(2, 0, 1, 3, 4), "y_hi")
    norm_block = trade_x(norm_block.transpose(2, 0, 1, 3, 4)).reshape(
        dp_count, 3, row_count, features
    )
    hidden_block = norm_block[:, 0].reshape(block_rows, features).astype(wide)
    resid_block = norm_block[:, 1].reshape(block_rows, features).astype(wide)
    scale_block = norm_block[:, 2, :, :3].astype(wide).reshape(block_rows, 3)
    scale_block = (scale_block[:, 0:1] + scale_block[:, 1:2]) + scale_block[:, 2:3]
    gain_block = lax.dynamic_slice_in_dim(
        norm_gain, lax.axis_index(dp_axes) * features, features, 0
    )
    normed = hidden_block * scale_block
    mlp_block = (normed * gain_block).astype(narrow)

    unit_group, mlp_block = lax.optimization_barrier((unit_group, mlp_block))
    shared_z = gather_z_relay(jnp.concatenate([mlp_block, join_weight]))
    unit_halves = (
        unit_group.reshape(z_count, 2, row_count, 2 * part_width)
        .transpose(1, 0, 2, 3)
        .reshape(2, plane_rows, 2 * part_width)
    )
    unit_halves = jnp.broadcast_to(
        unit_halves[None], (dp_count // core_count, core_count, plane_rows, 2 * part_width)
    ).reshape(dp_count, plane_rows, 2 * part_width)
    half_all = exchange(unit_halves, dp_axes).reshape(tokens, 2 * part_width)

    def both_near(own, near):
        both = jnp.pad(by_near(own, near), ((0, 0), (0, half_inputs), (0, 0)))
        return both.reshape(2 * part_width, features)

    weight_own = both_near(
        jnp.where(on_first, gate_weight, up_weight), jnp.where(on_first, near_gate, near_up)
    )
    weight_other = swap_cores(
        both_near(
            jnp.where(on_first, up_weight, gate_weight), jnp.where(on_first, near_up, near_gate)
        )
    )
    partial_other = jnp.dot(half_all, weight_other, preferred_element_type=wide)
    partial_own = jnp.dot(half_all, weight_own, preferred_element_type=wide)
    partial_value = partial_own + swap_cores(partial_other)
    partial_value = (
        partial_value.astype(narrow)
        .reshape(dp_count, z_count, row_count, features)
        .transpose(1, 0, 2, 3)
        .reshape(z_count, block_rows, features)
    )
    partial_value, shared_z = lax.optimization_barrier((partial_value, shared_z))
    join_z = shared_z[:, block_rows:]

    mlp_own = (
        from_first(shared_z[:, :block_rows])
        .reshape(z_count, dp_count, row_count, features)
        .transpose(1, 0, 2, 3)
        .reshape(tokens, features)
    )
    unit_sums = token_sum(half_all, jnp.concatenate([mlp_own, swap_cores(mlp_own)], axis=1))
    unit_sums = unit_sums.reshape(2, part_width, 2 * features)[:, :units]
    unit_kept = lax.dynamic_index_in_dim(unit_sums, here, 0, keepdims=False)
    unit_sent = lax.dynamic_index_in_dim(unit_sums, 1 - here, 0, keepdims=False)
    joined_half = jnp.concatenate(
        [half_all[:, units:part_width], half_all[:, part_width + units :]], axis=1
    )
    partial_far, unit_sent, joined_half, joined_other = lax.optimization_barrier(
        (
            exchange(partial_value, "z"),
            unit_sent.astype(narrow),
            joined_half,
            swap_cores(joined_half),
        )
    )
    unit_near = swap_near(unit_sent)
    input_grad = jnp.sum(partial_far.astype(wide), axis=0)

    lifted = input_grad * gain_block
    mean_part = jnp.sum(lifted * normed, axis=1)
    mean_all = exchange(
        jnp.broadcast_to(mean_part[None, None], (dp_count, 1, block_rows)), dp_axes
    )
    mean_all, unit_near = lax.optimization_barrier((mean_all, unit_near))
    inner_mean = (jnp.sum(mean_all, axis=(0, 1)) / width)[:, None]
    hidden_grad = (resid_block + scale_block * (lifted - normed * inner_mean)).astype(narrow)

    grad_rows = jnp.stack(
        [
            rows.reshape(dp_count, row_count, features)
            for rows in (hidden_grad, swap_near(hidden_grad))
        ],
        axis=1,
    ).reshape(2 * block_rows, features)
    joined_part = lax.dot_general(
        grad_rows, join_z, (((1,), (2,)), ((), ())), preferred_element_type=wide
    ).astype(narrow)
    joined_blocks = exchange(
        joined_part.reshape(dp_count, 2 * row_count, z_count * inputs), dp_axes
    )
    gain_part = jnp.sum(input_grad * normed, axis=0, keepdims=True)
    gain_part = gain_part + swap_near(gain_part)
    grad_sent = jnp.concatenate(
        [hidden_grad] + list(split_three(gain_part)) + [jnp.zeros((5, features), narrow)], axis=0
    )
    grad_z = gather_z(grad_sent)
    grad_z, joined_blocks = lax.optimization_barrier((grad_z, joined_blocks))
    joined_total = jnp.sum(joined_blocks.astype(wide), axis=0).astype(narrow)
    joined_total = joined_total.reshape(2, row_count, z_count, inputs).transpose(0, 2, 1, 3)
    joined_total = by_near(joined_total[0], swap_near(joined_total[1]))
    joined_grad = (
        from_first(joined_total.transpose(1, 0, 2, 3))
        .transpose(2, 1, 0, 3)
        .reshape(row_count, 2 * z_count * inputs)
    )

    gain_sum = jnp.sum(grad_z[:, block_rows : block_rows + 3].astype(wide), axis=(0, 1))
    gain_grad = exchange(
        jnp.broadcast_to(gain_sum[None, None], (dp_count, 1, features)), dp_axes
    ).reshape(width)
    grad_all = (
        grad_z[:, :block_rows]
        .reshape(z_count, dp_count, row_count, features)
        .transpose(1, 0, 2, 3)
        .reshape(tokens, features)
    )

    unit_grad = unit_kept + unit_near.astype(wide)
    own_grad = unit_grad[:, :features]
    other_grad = swap_cores(unit_grad[:, features:])
    gate_weight_grad = jnp.where(on_first, own_grad, other_grad)
    up_weight_grad = jnp.where(on_first, other_grad, own_grad)

    def add_near(sums):
        kept = lax.dynamic_index_in_dim(sums, here, 0, keepdims=False)
        sent = lax.dynamic_index_in_dim(sums, 1 - here, 0, keepdims=False)
        return kept + swap_near(sent)

    join_sums = by_core(
        token_sum(joined_half, grad_all).reshape(2, half_inputs, features),
        token_sum(joined_other, grad_all).reshape(2, half_inputs, features),
    )
    join_weight_grad = add_near(join_sums.transpose(1, 0, 2, 3)).reshape(inputs, features)
    return (joined_grad, gate_weight_grad, up_weight_grad, join_weight_grad, gain_grad)


def solution(mesh):
    tensor_count, dp_count = mesh.shape["tensor"], mesh.shape["dp"]
    fine = Mesh(
        mesh.devices.reshape(2, tensor_count // 2, dp_count // 4, 2, 2),
        ("y_lo", "z", "x", "y_hi", "core"),
    )
    tensor_axes = ("y_lo", "z")
    dp_axes = ("x", "y_hi", "core")
    rows = P(dp_axes + tensor_axes, None)
    blocks = P(tensor_axes, dp_axes)
    in_specs = (rows, rows, rows, rows, rows, rows, P(), blocks, blocks, blocks)
    out_specs = (rows, blocks, blocks, blocks, P())
    return jax.shard_map(shards, mesh=fine, in_specs=in_specs, out_specs=out_specs, check_vma=False)
```

```python
import jax
import jax.numpy as jnp
from jax import lax
from jax.sharding import Mesh
from jax.sharding import PartitionSpec as P

epsilon = 1e-05
narrow = jnp.bfloat16
wide = jnp.float32
z_axes = ("z_hi", "z_lo")


def swiglu_back(gate_act, up_act, product_grad):
    gate_wide = gate_act.astype(wide)
    logistic = jax.nn.sigmoid(gate_wide)
    product_wide = product_grad.astype(wide)
    gate_grad = (
        product_wide * up_act.astype(wide) * logistic * (1.0 + gate_wide * (1.0 - logistic))
    )
    up_grad = product_wide * gate_wide * logistic
    return (gate_grad.astype(narrow), up_grad.astype(narrow))


def token_sum(left, right):
    return lax.dot_general(left, right, (((0,), (0,)), ((), ())), preferred_element_type=wide)


def exchange(blocks, axes):
    return lax.all_to_all(blocks, axes, split_axis=0, concat_axis=0, tiled=True)


def swap_cores(value):
    return lax.ppermute(value, "core", [(0, 1), (1, 0)])


def swap_near(value):
    return lax.ppermute(value, "y_lo", [(0, 1), (1, 0)])


def from_above(value, distance, axes=z_axes):
    count = lax.axis_size(axes)
    return lax.ppermute(value, axes, [((i + distance) % count, i) for i in range(count)])


def gather_z(block):
    z_count = lax.axis_size(z_axes)
    quarter = z_count // 4
    strided = jnp.stack([block] + [from_above(block, 4 * step) for step in range(1, quarter)])
    below = from_above(strided, z_count - 1)
    below = jnp.concatenate([below[1:], below[:1]])
    all_blocks = jnp.stack(
        [strided, from_above(strided, 1), from_above(strided, 2), below], axis=1
    ).reshape(z_count, *block.shape)
    return from_first(all_blocks, z_axes)


def gather_ring(block, axis):
    count = lax.axis_size(axis)
    return jnp.stack([block] + [from_above(block, step, axis) for step in range(1, count)])


def from_first(blocks, axes):
    twice = jnp.concatenate([blocks, blocks])
    count = blocks.shape[0]
    return lax.dynamic_slice_in_dim(twice, count - lax.axis_index(axes), count, 0)


def trade_pair(blocks, axis_name):
    first = lax.axis_index(axis_name) == 0
    kept = jnp.where(first, blocks[0], blocks[1])
    sent = jnp.where(first, blocks[1], blocks[0])
    other = lax.ppermute(sent, axis_name, [(0, 1), (1, 0)])
    return jnp.stack([jnp.where(first, kept, other), jnp.where(first, other, kept)])


def trade_x(blocks):
    count, here = lax.axis_size("x"), lax.axis_index("x")
    turned = lax.dynamic_slice_in_dim(jnp.concatenate([blocks, blocks]), here, count, 0)
    pieces = [turned[0]] + [
        lax.ppermute(turned[step], "x", [(i, (i + step) % count) for i in range(count)])
        for step in range(1, count)
    ]
    back = jnp.stack([pieces[(count - step) % count] for step in range(count)])
    return lax.dynamic_slice_in_dim(jnp.concatenate([back, back]), count - here, count, 0)


def split_three(value):
    high = value.astype(narrow)
    rest = value - high.astype(wide)
    middle = rest.astype(narrow)
    low = (rest - middle.astype(wide)).astype(narrow)
    return (high, middle, low)


def shards(
    hidden,
    joined_in,
    gate_act,
    up_act,
    product_grad,
    resid_grad,
    norm_gain,
    gate_weight,
    up_weight,
    join_weight,
):
    dp_axes = ("x", "y_hi", "core")
    quarter = lax.axis_size("z_lo")
    z_count = lax.axis_size("z_hi") * quarter
    core_count = lax.axis_size("core")
    dp_count = lax.axis_size("x") * lax.axis_size("y_hi") * core_count
    row_count, width = hidden.shape
    units, features = gate_weight.shape
    inputs = join_weight.shape[0]
    half_inputs = inputs // 2
    part_width = units + half_inputs
    plane_rows = z_count * row_count
    block_rows = dp_count * row_count
    tokens = dp_count * plane_rows
    on_first = lax.axis_index("core") == 0
    here = lax.axis_index("y_lo")
    near_first = here == 0

    def by_near(own, near):
        return jnp.stack([jnp.where(near_first, own, near), jnp.where(near_first, near, own)])

    def by_core(own, other):
        return jnp.stack([jnp.where(on_first, own, other), jnp.where(on_first, other, own)])

    gate_grad, up_grad = swiglu_back(gate_act, up_act, product_grad)
    joined_rows = joined_in.reshape(row_count, 2, z_count, 2, half_inputs)
    gate_rows = jnp.concatenate(
        [gate_grad.reshape(row_count, 2, z_count, units), joined_rows[:, :, :, 0]], axis=3
    )
    up_rows = jnp.concatenate(
        [up_grad.reshape(row_count, 2, z_count, units), joined_rows[:, :, :, 1]], axis=3
    )
    unit_rows = jnp.stack([gate_rows, up_rows]).transpose(3, 0, 1, 2, 4)
    unit_rows = unit_rows.reshape(z_count, 2 * row_count, 2 * part_width)
    unit_rows, hidden, resid_grad = lax.optimization_barrier((unit_rows, hidden, resid_grad))
    unit_group = exchange(unit_rows, z_axes)

    hidden_wide = hidden.astype(wide)
    row_scale = lax.rsqrt(jnp.mean(hidden_wide * hidden_wide, axis=1, keepdims=True) + epsilon)
    scale_parts = jnp.concatenate(split_three(row_scale), axis=1)
    scale_parts = jnp.pad(scale_parts, ((0, 0), (0, features - scale_parts.shape[1])))
    norm_rows = jnp.stack(
        [
            hidden.reshape(row_count, dp_count, features),
            resid_grad.reshape(row_count, dp_count, features),
            jnp.broadcast_to(scale_parts[:, None, :], (row_count, dp_count, features)),
        ]
    )
    norm_sent = norm_rows.transpose(2, 0, 1, 3).reshape(
        lax.axis_size("x"), 2, 2, 3 * row_count, features
    )
    norm_block = trade_pair(norm_sent.transpose(2, 0, 1, 3, 4), "core")
    norm_block, near_weights = lax.optimization_barrier(
        (norm_block, swap_near(jnp.stack([gate_weight, up_weight])))
    )
    near_gate, near_up = near_weights[0], near_weights[1]
    norm_block = trade_pair(norm_block.transpose(2, 0, 1, 3, 4), "y_hi")
    norm_block = trade_x(norm_block.transpose(2, 0, 1, 3, 4)).reshape(
        dp_count, 3, row_count, features
    )
    hidden_block = norm_block[:, 0].reshape(block_rows, features).astype(wide)
    resid_block = norm_block[:, 1].reshape(block_rows, features).astype(wide)
    scale_block = norm_block[:, 2, :, :3].astype(wide).reshape(block_rows, 3)
    scale_block = (scale_block[:, 0:1] + scale_block[:, 1:2]) + scale_block[:, 2:3]
    gain_block = lax.dynamic_slice_in_dim(
        norm_gain, lax.axis_index(dp_axes) * features, features, 0
    )
    normed = hidden_block * scale_block
    mlp_block = (normed * gain_block).astype(narrow)

    unit_group, mlp_block = lax.optimization_barrier((unit_group, mlp_block))
    mlp_z = gather_z(mlp_block)
    unit_halves = (
        unit_group.reshape(z_count, 2, row_count, 2 * part_width)
        .transpose(1, 0, 2, 3)
        .reshape(2, plane_rows, 2 * part_width)
    )
    unit_halves = jnp.broadcast_to(
        unit_halves[None], (dp_count // core_count, core_count, plane_rows, 2 * part_width)
    ).reshape(dp_count, plane_rows, 2 * part_width)
    half_all = exchange(unit_halves, dp_axes).reshape(tokens, 2 * part_width)
    join_quad = gather_ring(join_weight, "z_lo")
    half_all, mlp_z, join_quad = lax.optimization_barrier((half_all, mlp_z, join_quad))

    def both_near(own, near):
        both = jnp.pad(by_near(own, near), ((0, 0), (0, half_inputs), (0, 0)))
        return both.reshape(2 * part_width, features)

    weight_own = both_near(
        jnp.where(on_first, gate_weight, up_weight), jnp.where(on_first, near_gate, near_up)
    )
    weight_other = swap_cores(
        both_near(
            jnp.where(on_first, up_weight, gate_weight), jnp.where(on_first, near_up, near_gate)
        )
    )
    partial_other = jnp.dot(half_all, weight_other, preferred_element_type=wide)
    partial_own = jnp.dot(half_all, weight_own, preferred_element_type=wide)
    partial_value = partial_own + swap_cores(partial_other)
    partial_value = (
        partial_value.astype(narrow)
        .reshape(dp_count, z_count, row_count, features)
        .transpose(1, 0, 2, 3)
        .reshape(z_count, block_rows, features)
    )

    mlp_own = (
        mlp_z.reshape(z_count, dp_count, row_count, features)
        .transpose(1, 0, 2, 3)
        .reshape(tokens, features)
    )
    unit_sums = token_sum(half_all, jnp.concatenate([mlp_own, swap_cores(mlp_own)], axis=1))
    unit_sums = unit_sums.reshape(2, part_width, 2 * features)[:, :units]
    unit_kept = lax.dynamic_index_in_dim(unit_sums, here, 0, keepdims=False)
    unit_sent = lax.dynamic_index_in_dim(unit_sums, 1 - here, 0, keepdims=False)
    joined_half = jnp.concatenate(
        [half_all[:, units:part_width], half_all[:, part_width + units :]], axis=1
    )
    partial_far, unit_sent, joined_half, joined_other, near_quad = lax.optimization_barrier(
        (
            exchange(partial_value, z_axes),
            unit_sent.astype(narrow),
            joined_half,
            swap_cores(joined_half),
            swap_near(join_quad),
        )
    )
    unit_near = swap_near(unit_sent)
    input_grad = jnp.sum(partial_far.astype(wide), axis=0)

    lifted = input_grad * gain_block
    mean_part = jnp.sum(lifted * normed, axis=1)
    gain_part = jnp.sum(input_grad * normed, axis=0)
    row_parts = jnp.concatenate([mean_part, gain_part])
    row_parts = exchange(
        jnp.broadcast_to(row_parts[None, None], (dp_count, 1, block_rows + features)), dp_axes
    )[:, 0]
    inner_mean = (jnp.sum(row_parts[:, :block_rows], axis=0) / width)[:, None]
    gain_part = row_parts[:, block_rows:]
    hidden_grad = (resid_block + scale_block * (lifted - normed * inner_mean)).astype(narrow)

    grad_sent = jnp.concatenate([hidden_grad, *split_three(gain_part)])
    sent_rows = block_rows + 3 * dp_count
    high_count = z_count // quarter
    grad_high = exchange(
        jnp.broadcast_to(grad_sent[None], (high_count, sent_rows, features)), "z_hi"
    )

    join_pair = by_near(join_quad, near_quad).reshape(2 * quarter * inputs, features)
    joined_half, joined_other = joined_half.T, joined_other.T
    grad_high, unit_near, join_pair, joined_half, joined_other = lax.optimization_barrier(
        (grad_high, unit_near, join_pair, joined_half, joined_other)
    )

    grad_rows = (
        grad_high[:, :block_rows]
        .reshape(high_count, dp_count, row_count, features)
        .transpose(1, 0, 2, 3)
        .reshape(dp_count * high_count * row_count, features)
    )
    joined_part = lax.dot_general(
        grad_rows, join_pair, (((1,), (1,)), ((), ())), preferred_element_type=wide
    ).astype(narrow)
    joined_blocks = exchange(
        joined_part.reshape(dp_count, high_count * row_count, 2 * quarter * inputs), dp_axes
    )
    unit_grad = unit_kept + unit_near.astype(wide)
    other_grad = swap_cores(unit_grad[:, features:])

    def sum_parts(blocks):
        parts = jnp.sum(blocks.astype(wide).reshape(-1, 3, dp_count, features), axis=0)
        return (parts[0] + parts[1]) + parts[2]

    gain_high = sum_parts(grad_high[:, block_rows:])
    gain_high = gain_high + swap_near(gain_high)
    grad_quad = jnp.concatenate(
        [grad_high[:, :block_rows].reshape(-1, features), *split_three(gain_high)]
    )
    grad_z = from_first(gather_ring(grad_quad, "z_lo"), "z_lo")
    grad_z, joined_blocks = lax.optimization_barrier((grad_z, joined_blocks))
    joined_total = jnp.sum(joined_blocks.astype(wide), axis=0).astype(narrow)
    joined_high = exchange(
        joined_total.reshape(high_count, row_count, 2 * quarter * inputs), "z_hi"
    ).reshape(high_count, row_count, 2, quarter, inputs)
    joined_grad = (
        from_first(joined_high.transpose(3, 0, 1, 2, 4), "z_lo")
        .transpose(2, 3, 1, 0, 4)
        .reshape(row_count, 2 * z_count * inputs)
    )

    high_rows = high_count * block_rows
    gain_grad = sum_parts(grad_z[:, high_rows:]).reshape(width)
    grad_all = (
        grad_z[:, :high_rows]
        .reshape(quarter, high_count, dp_count, row_count, features)
        .transpose(2, 1, 0, 3, 4)
        .reshape(tokens, features)
    )

    own_grad = unit_grad[:, :features]
    gate_weight_grad = jnp.where(on_first, own_grad, other_grad)
    up_weight_grad = jnp.where(on_first, other_grad, own_grad)

    def add_near(sums):
        kept = lax.dynamic_index_in_dim(sums, here, 0, keepdims=False)
        sent = lax.dynamic_index_in_dim(sums, 1 - here, 0, keepdims=False)
        return kept + swap_near(sent)

    join_sums = by_core(
        jnp.dot(joined_half, grad_all, preferred_element_type=wide).reshape(2, half_inputs, features),
        jnp.dot(joined_other, grad_all, preferred_element_type=wide).reshape(2, half_inputs, features),
    )
    join_weight_grad = add_near(join_sums.transpose(1, 0, 2, 3)).reshape(inputs, features)
    return (joined_grad, gate_weight_grad, up_weight_grad, join_weight_grad, gain_grad)


def solution(mesh):
    tensor_count, dp_count = mesh.shape["tensor"], mesh.shape["dp"]
    fine = Mesh(
        mesh.devices.reshape(2, tensor_count // 8, 4, dp_count // 4, 2, 2),
        ("y_lo", "z_hi", "z_lo", "x", "y_hi", "core"),
    )
    tensor_axes = ("y_lo",) + z_axes
    dp_axes = ("x", "y_hi", "core")
    rows = P(dp_axes + tensor_axes, None)
    blocks = P(tensor_axes, dp_axes)
    in_specs = (rows, rows, rows, rows, rows, rows, P(), blocks, blocks, blocks)
    out_specs = (rows, blocks, blocks, blocks, P())
    return jax.shard_map(shards, mesh=fine, in_specs=in_specs, out_specs=out_specs, check_vma=False)
```

```python
import jax
import jax.numpy as jnp
from jax import lax
from jax.sharding import Mesh
from jax.sharding import PartitionSpec as P

epsilon = 1e-05
narrow = jnp.bfloat16
wide = jnp.float32
z_axes = ("z_hi", "z_lo")


def swiglu_back(gate_act, up_act, product_grad):
    gate_wide = gate_act.astype(wide)
    logistic = jax.nn.sigmoid(gate_wide)
    product_wide = product_grad.astype(wide)
    gate_grad = (
        product_wide * up_act.astype(wide) * logistic * (1.0 + gate_wide * (1.0 - logistic))
    )
    up_grad = product_wide * gate_wide * logistic
    return (gate_grad.astype(narrow), up_grad.astype(narrow))


def token_sum(left, right):
    return lax.dot_general(left, right, (((0,), (0,)), ((), ())), preferred_element_type=wide)


def exchange(blocks, axes):
    return lax.all_to_all(blocks, axes, split_axis=0, concat_axis=0, tiled=True)


def swap_cores(value):
    return lax.ppermute(value, "core", [(0, 1), (1, 0)])


def swap_near(value):
    return lax.ppermute(value, "y_lo", [(0, 1), (1, 0)])


def from_above(value, distance, axes=z_axes):
    count = lax.axis_size(axes)
    return lax.ppermute(value, axes, [((i + distance) % count, i) for i in range(count)])


def gather_z(block):
    z_count = lax.axis_size(z_axes)
    quarter = z_count // 4
    strided = jnp.stack([block] + [from_above(block, 4 * step) for step in range(1, quarter)])
    below = from_above(strided, z_count - 1)
    below = jnp.concatenate([below[1:], below[:1]])
    all_blocks = jnp.stack(
        [strided, from_above(strided, 1), from_above(strided, 2), below], axis=1
    ).reshape(z_count, *block.shape)
    return from_first(all_blocks, z_axes)


def gather_ring(block, axis):
    count = lax.axis_size(axis)
    return jnp.stack([block] + [from_above(block, step, axis) for step in range(1, count)])


def from_first(blocks, axes):
    twice = jnp.concatenate([blocks, blocks])
    count = blocks.shape[0]
    return lax.dynamic_slice_in_dim(twice, count - lax.axis_index(axes), count, 0)


def trade_pair(blocks, axis_name):
    first = lax.axis_index(axis_name) == 0
    kept = jnp.where(first, blocks[0], blocks[1])
    sent = jnp.where(first, blocks[1], blocks[0])
    other = lax.ppermute(sent, axis_name, [(0, 1), (1, 0)])
    return jnp.stack([jnp.where(first, kept, other), jnp.where(first, other, kept)])


def trade_x(blocks):
    count, here = lax.axis_size("x"), lax.axis_index("x")
    turned = lax.dynamic_slice_in_dim(jnp.concatenate([blocks, blocks]), here, count, 0)
    pieces = [turned[0]] + [
        lax.ppermute(turned[step], "x", [(i, (i + step) % count) for i in range(count)])
        for step in range(1, count)
    ]
    back = jnp.stack([pieces[(count - step) % count] for step in range(count)])
    return lax.dynamic_slice_in_dim(jnp.concatenate([back, back]), count - here, count, 0)


def split_three(value):
    high = value.astype(narrow)
    rest = value - high.astype(wide)
    middle = rest.astype(narrow)
    low = (rest - middle.astype(wide)).astype(narrow)
    return (high, middle, low)


def split_two(value):
    high = value.astype(narrow)
    return (high, (value - high.astype(wide)).astype(narrow))


def shards(
    hidden,
    joined_in,
    gate_act,
    up_act,
    product_grad,
    resid_grad,
    norm_gain,
    gate_weight,
    up_weight,
    join_weight,
):
    dp_axes = ("x", "y_hi", "core")
    quarter = lax.axis_size("z_lo")
    z_count = lax.axis_size("z_hi") * quarter
    core_count = lax.axis_size("core")
    dp_count = lax.axis_size("x") * lax.axis_size("y_hi") * core_count
    row_count, width = hidden.shape
    units, features = gate_weight.shape
    inputs = join_weight.shape[0]
    half_inputs = inputs // 2
    part_width = units + half_inputs
    plane_rows = z_count * row_count
    block_rows = dp_count * row_count
    tokens = dp_count * plane_rows
    on_first = lax.axis_index("core") == 0
    here = lax.axis_index("y_lo")
    near_first = here == 0

    def by_near(own, near):
        return jnp.stack([jnp.where(near_first, own, near), jnp.where(near_first, near, own)])

    def by_core(own, other):
        return jnp.stack([jnp.where(on_first, own, other), jnp.where(on_first, other, own)])

    gate_grad, up_grad = swiglu_back(gate_act, up_act, product_grad)
    joined_rows = joined_in.reshape(row_count, 2, z_count, 2, half_inputs)
    gate_rows = jnp.concatenate(
        [gate_grad.reshape(row_count, 2, z_count, units), joined_rows[:, :, :, 0]], axis=3
    )
    up_rows = jnp.concatenate(
        [up_grad.reshape(row_count, 2, z_count, units), joined_rows[:, :, :, 1]], axis=3
    )
    unit_rows = jnp.stack([gate_rows, up_rows]).transpose(3, 0, 1, 2, 4)
    unit_rows = unit_rows.reshape(z_count, 2 * row_count, 2 * part_width)
    unit_rows, hidden, resid_grad = lax.optimization_barrier((unit_rows, hidden, resid_grad))
    unit_group = exchange(unit_rows, z_axes)

    hidden_wide = hidden.astype(wide)
    row_scale = lax.rsqrt(jnp.mean(hidden_wide * hidden_wide, axis=1, keepdims=True) + epsilon)
    scale_parts = jnp.concatenate(split_three(row_scale), axis=1)
    scale_parts = jnp.pad(scale_parts, ((0, 0), (0, features - scale_parts.shape[1])))
    norm_rows = jnp.stack(
        [
            hidden.reshape(row_count, dp_count, features),
            resid_grad.reshape(row_count, dp_count, features),
            jnp.broadcast_to(scale_parts[:, None, :], (row_count, dp_count, features)),
        ]
    )
    norm_sent = norm_rows.transpose(2, 0, 1, 3).reshape(
        lax.axis_size("x"), 2, 2, 3 * row_count, features
    )
    norm_block = trade_pair(norm_sent.transpose(2, 0, 1, 3, 4), "core")
    norm_block, near_weights = lax.optimization_barrier(
        (norm_block, swap_near(jnp.stack([gate_weight, up_weight])))
    )
    near_gate, near_up = near_weights[0], near_weights[1]
    norm_block = trade_pair(norm_block.transpose(2, 0, 1, 3, 4), "y_hi")
    norm_block = trade_x(norm_block.transpose(2, 0, 1, 3, 4)).reshape(
        dp_count, 3, row_count, features
    )
    hidden_block = norm_block[:, 0].reshape(block_rows, features).astype(wide)
    resid_block = norm_block[:, 1].reshape(block_rows, features).astype(wide)
    scale_block = norm_block[:, 2, :, :3].astype(wide).reshape(block_rows, 3)
    scale_block = (scale_block[:, 0:1] + scale_block[:, 1:2]) + scale_block[:, 2:3]
    gain_block = lax.dynamic_slice_in_dim(
        norm_gain, lax.axis_index(dp_axes) * features, features, 0
    )
    normed = hidden_block * scale_block
    mlp_block = (normed * gain_block).astype(narrow)

    unit_group, mlp_block = lax.optimization_barrier((unit_group, mlp_block))
    mlp_z = gather_z(mlp_block)
    unit_halves = (
        unit_group.reshape(z_count, 2, row_count, 2 * part_width)
        .transpose(1, 0, 2, 3)
        .reshape(2, plane_rows, 2 * part_width)
    )
    unit_halves = jnp.broadcast_to(
        unit_halves[None], (dp_count // core_count, core_count, plane_rows, 2 * part_width)
    ).reshape(dp_count, plane_rows, 2 * part_width)
    half_all = exchange(unit_halves, dp_axes).reshape(tokens, 2 * part_width)
    join_quad = gather_ring(join_weight, "z_lo")
    half_all, mlp_z, join_quad = lax.optimization_barrier((half_all, mlp_z, join_quad))

    def both_near(own, near):
        both = jnp.pad(by_near(own, near), ((0, 0), (0, half_inputs), (0, 0)))
        return both.reshape(2 * part_width, features)

    weight_own = both_near(
        jnp.where(on_first, gate_weight, up_weight), jnp.where(on_first, near_gate, near_up)
    )
    weight_other = swap_cores(
        both_near(
            jnp.where(on_first, up_weight, gate_weight), jnp.where(on_first, near_up, near_gate)
        )
    )
    partial_other = jnp.dot(half_all, weight_other, preferred_element_type=wide)
    partial_own = jnp.dot(half_all, weight_own, preferred_element_type=wide)
    partial_value = partial_own + swap_cores(partial_other)
    partial_value = (
        partial_value.astype(narrow)
        .reshape(dp_count, z_count, row_count, features)
        .transpose(1, 0, 2, 3)
        .reshape(z_count, block_rows, features)
    )

    mlp_own = (
        mlp_z.reshape(z_count, dp_count, row_count, features)
        .transpose(1, 0, 2, 3)
        .reshape(tokens, features)
    )
    unit_sums = token_sum(half_all, jnp.concatenate([mlp_own, swap_cores(mlp_own)], axis=1))
    unit_sums = unit_sums.reshape(2, part_width, 2 * features)[:, :units]
    unit_kept = lax.dynamic_index_in_dim(unit_sums, here, 0, keepdims=False)
    unit_sent = lax.dynamic_index_in_dim(unit_sums, 1 - here, 0, keepdims=False)
    joined_half = jnp.concatenate(
        [half_all[:, units:part_width], half_all[:, part_width + units :]], axis=1
    )
    partial_far, unit_sent, joined_half, joined_other, near_quad = lax.optimization_barrier(
        (
            exchange(partial_value, z_axes),
            unit_sent.astype(narrow),
            joined_half,
            swap_cores(joined_half),
            swap_near(join_quad),
        )
    )
    unit_near = swap_near(unit_sent)
    input_grad = jnp.sum(partial_far.astype(wide), axis=0)

    lifted = input_grad * gain_block
    mean_part = jnp.sum(lifted * normed, axis=1)
    gain_part = jnp.sum(input_grad * normed, axis=0)
    row_parts = jnp.concatenate([mean_part, gain_part])
    row_parts = exchange(
        jnp.broadcast_to(row_parts[None, None], (dp_count, 1, block_rows + features)), dp_axes
    )[:, 0]
    inner_mean = (jnp.sum(row_parts[:, :block_rows], axis=0) / width)[:, None]
    gain_part = row_parts[:, block_rows:]
    hidden_grad = (resid_block + scale_block * (lifted - normed * inner_mean)).astype(narrow)

    grad_sent = jnp.concatenate([hidden_grad, *split_two(gain_part)])
    sent_rows = block_rows + 2 * dp_count
    high_count = z_count // quarter
    grad_high = exchange(
        jnp.broadcast_to(grad_sent[None], (high_count, sent_rows, features)), "z_hi"
    )

    join_pair = by_near(join_quad, near_quad).reshape(2 * quarter * inputs, features)
    joined_half, joined_other = joined_half.T, joined_other.T
    unit_grad = unit_kept + unit_near.astype(wide)
    grad_high, own_grad, other_sent, join_pair, joined_half, joined_other = (
        lax.optimization_barrier(
            (
                grad_high,
                unit_grad[:, :features],
                unit_grad[:, features:],
                join_pair,
                joined_half,
                joined_other,
            )
        )
    )

    grad_rows = (
        grad_high[:, :block_rows]
        .reshape(high_count, dp_count, row_count, features)
        .transpose(1, 0, 2, 3)
        .reshape(dp_count * high_count * row_count, features)
    )
    joined_part = lax.dot_general(
        grad_rows, join_pair, (((1,), (1,)), ((), ())), preferred_element_type=wide
    ).astype(narrow)
    joined_blocks = exchange(
        joined_part.reshape(dp_count, high_count * row_count, 2 * quarter * inputs), dp_axes
    )
    grad_high, other_grad = lax.optimization_barrier((grad_high, swap_cores(other_sent)))
    gate_weight_grad = jnp.where(on_first, own_grad, other_grad)
    up_weight_grad = jnp.where(on_first, other_grad, own_grad)

    def sum_parts(blocks):
        parts = jnp.sum(blocks.astype(wide).reshape(-1, 2, dp_count, features), axis=0)
        return parts[0] + parts[1]

    gain_high = sum_parts(grad_high[:, block_rows:])
    grad_quad = jnp.concatenate(
        [grad_high[:, :block_rows].reshape(-1, features), *split_two(gain_high)]
    )
    grad_z = from_first(gather_ring(grad_quad, "z_lo"), "z_lo")
    grad_z, joined_blocks = lax.optimization_barrier((grad_z, joined_blocks))
    joined_total = jnp.sum(joined_blocks.astype(wide), axis=0).astype(narrow)
    joined_high = exchange(
        joined_total.reshape(high_count, row_count, 2 * quarter * inputs), "z_hi"
    ).reshape(high_count, row_count, 2, quarter, inputs)
    joined_grad = (
        from_first(joined_high.transpose(3, 0, 1, 2, 4), "z_lo")
        .transpose(2, 3, 1, 0, 4)
        .reshape(row_count, 2 * z_count * inputs)
    )

    high_rows = high_count * block_rows
    gain_sum = sum_parts(grad_z[:, high_rows:])
    gain_grad = (gain_sum + swap_near(gain_sum)).reshape(width)
    grad_all = (
        grad_z[:, :high_rows]
        .reshape(quarter, high_count, dp_count, row_count, features)
        .transpose(2, 1, 0, 3, 4)
        .reshape(tokens, features)
    )

    def add_near(sums):
        kept = lax.dynamic_index_in_dim(sums, here, 0, keepdims=False)
        sent = lax.dynamic_index_in_dim(sums, 1 - here, 0, keepdims=False)
        return kept + swap_near(sent)

    join_sums = by_core(
        jnp.dot(joined_half, grad_all, preferred_element_type=wide).reshape(2, half_inputs, features),
        jnp.dot(joined_other, grad_all, preferred_element_type=wide).reshape(2, half_inputs, features),
    )
    join_weight_grad = add_near(join_sums.transpose(1, 0, 2, 3)).reshape(inputs, features)
    return (joined_grad, gate_weight_grad, up_weight_grad, join_weight_grad, gain_grad)


def solution(mesh):
    tensor_count, dp_count = mesh.shape["tensor"], mesh.shape["dp"]
    fine = Mesh(
        mesh.devices.reshape(2, tensor_count // 8, 4, dp_count // 4, 2, 2),
        ("y_lo", "z_hi", "z_lo", "x", "y_hi", "core"),
    )
    tensor_axes = ("y_lo",) + z_axes
    dp_axes = ("x", "y_hi", "core")
    rows = P(dp_axes + tensor_axes, None)
    blocks = P(tensor_axes, dp_axes)
    in_specs = (rows, rows, rows, rows, rows, rows, P(), blocks, blocks, blocks)
    out_specs = (rows, blocks, blocks, blocks, P())
    return jax.shard_map(shards, mesh=fine, in_specs=in_specs, out_specs=out_specs, check_vma=False)
```

```python
import jax
import jax.numpy as jnp
from jax import lax
from jax.sharding import Mesh
from jax.sharding import PartitionSpec as P

epsilon = 1e-05
narrow = jnp.bfloat16
wide = jnp.float32
z_axes = ("z_top", "z_mid", "z_lo")


def swiglu_back(gate_act, up_act, product_grad):
    gate_wide = gate_act.astype(wide)
    logistic = jax.nn.sigmoid(gate_wide)
    product_wide = product_grad.astype(wide)
    gate_grad = (
        product_wide * up_act.astype(wide) * logistic * (1.0 + gate_wide * (1.0 - logistic))
    )
    up_grad = product_wide * gate_wide * logistic
    return (gate_grad.astype(narrow), up_grad.astype(narrow))


def token_sum(left, right):
    return lax.dot_general(left, right, (((0,), (0,)), ((), ())), preferred_element_type=wide)


def exchange(blocks, axes):
    return lax.all_to_all(blocks, axes, split_axis=0, concat_axis=0, tiled=True)


def swap_cores(value):
    return lax.ppermute(value, "core", [(0, 1), (1, 0)])


def swap_near(value):
    return lax.ppermute(value, "y_lo", [(0, 1), (1, 0)])


def from_above(value, distance, axes=z_axes):
    count = lax.axis_size(axes)
    return lax.ppermute(value, axes, [((i + distance) % count, i) for i in range(count)])


def gather_far(block):
    quarter = lax.axis_size(z_axes) // 4
    return jnp.stack([block] + [from_above(block, 4 * step) for step in range(1, quarter)])


def gather_near(strided):
    z_count = lax.axis_size(z_axes)
    below = from_above(strided, z_count - 1)
    below = jnp.concatenate([below[1:], below[:1]])
    all_blocks = jnp.stack(
        [strided, from_above(strided, 1), from_above(strided, 2), below], axis=1
    ).reshape(z_count, *strided.shape[1:])
    return from_first(all_blocks, z_axes)


def gather_ring(block, axis):
    count = lax.axis_size(axis)
    return jnp.stack([block] + [from_above(block, step, axis) for step in range(1, count)])


def from_first(blocks, axes):
    twice = jnp.concatenate([blocks, blocks])
    count = blocks.shape[0]
    return lax.dynamic_slice_in_dim(twice, count - lax.axis_index(axes), count, 0)


def gather_pair(block, axis):
    first = lax.axis_index(axis) == 0
    other = lax.ppermute(block, axis, [(0, 1), (1, 0)])
    return jnp.stack([jnp.where(first, block, other), jnp.where(first, other, block)])


def trade_pair(blocks, axis_name):
    first = lax.axis_index(axis_name) == 0
    kept = jnp.where(first, blocks[0], blocks[1])
    sent = jnp.where(first, blocks[1], blocks[0])
    other = lax.ppermute(sent, axis_name, [(0, 1), (1, 0)])
    return jnp.stack([jnp.where(first, kept, other), jnp.where(first, other, kept)])


def trade_x(blocks):
    count, here = lax.axis_size("x"), lax.axis_index("x")
    turned = lax.dynamic_slice_in_dim(jnp.concatenate([blocks, blocks]), here, count, 0)
    pieces = [turned[0]] + [
        lax.ppermute(turned[step], "x", [(i, (i + step) % count) for i in range(count)])
        for step in range(1, count)
    ]
    back = jnp.stack([pieces[(count - step) % count] for step in range(count)])
    return lax.dynamic_slice_in_dim(jnp.concatenate([back, back]), count - here, count, 0)


def split_three(value):
    high = value.astype(narrow)
    rest = value - high.astype(wide)
    middle = rest.astype(narrow)
    low = (rest - middle.astype(wide)).astype(narrow)
    return (high, middle, low)


def split_two(value):
    high = value.astype(narrow)
    return (high, (value - high.astype(wide)).astype(narrow))


def shards(
    hidden,
    joined_in,
    gate_act,
    up_act,
    product_grad,
    resid_grad,
    norm_gain,
    gate_weight,
    up_weight,
    join_weight,
):
    dp_axes = ("x", "y_hi", "core")
    quarter = lax.axis_size("z_lo")
    z_count = 4 * quarter
    core_count = lax.axis_size("core")
    dp_count = lax.axis_size("x") * lax.axis_size("y_hi") * core_count
    row_count, width = hidden.shape
    units, features = gate_weight.shape
    inputs = join_weight.shape[0]
    half_inputs = inputs // 2
    part_width = units + half_inputs
    plane_rows = z_count * row_count
    block_rows = dp_count * row_count
    tokens = dp_count * plane_rows
    on_first = lax.axis_index("core") == 0
    here = lax.axis_index("y_lo")
    near_first = here == 0

    def by_near(own, near):
        return jnp.stack([jnp.where(near_first, own, near), jnp.where(near_first, near, own)])

    def by_core(own, other):
        return jnp.stack([jnp.where(on_first, own, other), jnp.where(on_first, other, own)])

    gate_grad, up_grad = swiglu_back(gate_act, up_act, product_grad)
    joined_rows = joined_in.reshape(row_count, 2, z_count, 2, half_inputs)
    gate_rows = jnp.concatenate(
        [gate_grad.reshape(row_count, 2, z_count, units), joined_rows[:, :, :, 0]], axis=3
    )
    up_rows = jnp.concatenate(
        [up_grad.reshape(row_count, 2, z_count, units), joined_rows[:, :, :, 1]], axis=3
    )
    unit_rows = jnp.stack([gate_rows, up_rows]).transpose(3, 0, 1, 2, 4)
    unit_rows = unit_rows.reshape(z_count, 2 * row_count, 2 * part_width)
    unit_rows, hidden, resid_grad = lax.optimization_barrier((unit_rows, hidden, resid_grad))
    unit_group = exchange(unit_rows, z_axes)

    hidden_wide = hidden.astype(wide)
    row_scale = lax.rsqrt(jnp.mean(hidden_wide * hidden_wide, axis=1, keepdims=True) + epsilon)
    scale_parts = jnp.concatenate(split_three(row_scale), axis=1)
    scale_parts = jnp.pad(scale_parts, ((0, 0), (0, features - scale_parts.shape[1])))
    norm_rows = jnp.stack(
        [
            hidden.reshape(row_count, dp_count, features),
            resid_grad.reshape(row_count, dp_count, features),
            jnp.broadcast_to(scale_parts[:, None, :], (row_count, dp_count, features)),
        ]
    )
    norm_sent = norm_rows.transpose(2, 0, 1, 3).reshape(
        lax.axis_size("x"), 2, 2, 3 * row_count, features
    )
    norm_block = trade_pair(norm_sent.transpose(2, 0, 1, 3, 4), "core")
    norm_block, near_weights = lax.optimization_barrier(
        (norm_block, swap_near(jnp.stack([gate_weight, up_weight])))
    )
    near_gate, near_up = near_weights[0], near_weights[1]
    norm_block = trade_pair(norm_block.transpose(2, 0, 1, 3, 4), "y_hi")
    norm_block = trade_x(norm_block.transpose(2, 0, 1, 3, 4)).reshape(
        dp_count, 3, row_count, features
    )
    hidden_block = norm_block[:, 0].reshape(block_rows, features).astype(wide)
    resid_block = norm_block[:, 1].reshape(block_rows, features).astype(wide)
    scale_block = norm_block[:, 2, :, :3].astype(wide).reshape(block_rows, 3)
    scale_block = (scale_block[:, 0:1] + scale_block[:, 1:2]) + scale_block[:, 2:3]
    gain_block = lax.dynamic_slice_in_dim(
        norm_gain, lax.axis_index(dp_axes) * features, features, 0
    )
    normed = hidden_block * scale_block
    mlp_block = (normed * gain_block).astype(narrow)

    unit_group, mlp_block = lax.optimization_barrier((unit_group, mlp_block))
    mlp_far, join_pair = lax.optimization_barrier(
        (gather_far(mlp_block), gather_pair(join_weight, "z_mid"))
    )
    mlp_z, join_quad = gather_near(mlp_far), gather_ring(join_pair, "z_lo")
    unit_halves = (
        unit_group.reshape(z_count, 2, row_count, 2 * part_width)
        .transpose(1, 0, 2, 3)
        .reshape(2, plane_rows, 2 * part_width)
    )
    unit_halves = jnp.broadcast_to(
        unit_halves[None], (dp_count // core_count, core_count, plane_rows, 2 * part_width)
    ).reshape(dp_count, plane_rows, 2 * part_width)
    half_all = exchange(unit_halves, dp_axes).reshape(tokens, 2 * part_width)
    half_all, mlp_z, join_quad = lax.optimization_barrier((half_all, mlp_z, join_quad))

    def both_near(own, near):
        both = jnp.pad(by_near(own, near), ((0, 0), (0, half_inputs), (0, 0)))
        return both.reshape(2 * part_width, features)

    weight_own = both_near(
        jnp.where(on_first, gate_weight, up_weight), jnp.where(on_first, near_gate, near_up)
    )
    weight_other = swap_cores(
        both_near(
            jnp.where(on_first, up_weight, gate_weight), jnp.where(on_first, near_up, near_gate)
        )
    )
    partial_other = jnp.dot(half_all, weight_other, preferred_element_type=wide)
    partial_own = jnp.dot(half_all, weight_own, preferred_element_type=wide)
    partial_value = partial_own + swap_cores(partial_other)
    partial_value = (
        partial_value.astype(narrow)
        .reshape(dp_count, z_count, row_count, features)
        .transpose(1, 0, 2, 3)
        .reshape(z_count, block_rows, features)
    )

    mlp_own = (
        mlp_z.reshape(z_count, dp_count, row_count, features)
        .transpose(1, 0, 2, 3)
        .reshape(tokens, features)
    )
    unit_sums = token_sum(half_all, jnp.concatenate([mlp_own, swap_cores(mlp_own)], axis=1))
    unit_sums = unit_sums.reshape(2, part_width, 2 * features)[:, :units]
    unit_kept = lax.dynamic_index_in_dim(unit_sums, here, 0, keepdims=False)
    unit_sent = lax.dynamic_index_in_dim(unit_sums, 1 - here, 0, keepdims=False)
    joined_half = jnp.concatenate(
        [half_all[:, units:part_width], half_all[:, part_width + units :]], axis=1
    )
    partial_far, unit_sent, joined_half, joined_other, near_quad = lax.optimization_barrier(
        (
            exchange(partial_value, z_axes),
            unit_sent.astype(narrow),
            joined_half,
            swap_cores(joined_half),
            swap_near(join_quad),
        )
    )
    unit_near = swap_near(unit_sent)
    input_grad = jnp.sum(partial_far.astype(wide), axis=0)

    lifted = input_grad * gain_block
    mean_part = jnp.sum(lifted * normed, axis=1)
    gain_part = jnp.sum(input_grad * normed, axis=0)
    row_parts = jnp.concatenate([mean_part, gain_part])
    row_parts = exchange(
        jnp.broadcast_to(row_parts[None, None], (dp_count, 1, block_rows + features)), dp_axes
    )[:, 0]
    inner_mean = (jnp.sum(row_parts[:, :block_rows], axis=0) / width)[:, None]
    gain_part = row_parts[:, block_rows:]
    hidden_grad = (resid_block + scale_block * (lifted - normed * inner_mean)).astype(narrow)

    grad_sent = jnp.concatenate([hidden_grad, *split_two(gain_part)])
    sent_rows = block_rows + 2 * dp_count
    high_count = 2
    grad_high = gather_pair(grad_sent, "z_top")

    join_pair = by_near(join_quad, near_quad).reshape(4 * quarter * inputs, features)
    joined_half, joined_other = joined_half.T, joined_other.T
    grad_high, join_pair, joined_half, joined_other = lax.optimization_barrier(
        (grad_high, join_pair, joined_half, joined_other)
    )

    grad_rows = (
        grad_high[:, :block_rows]
        .reshape(high_count, dp_count, row_count, features)
        .transpose(1, 0, 2, 3)
        .reshape(dp_count * high_count * row_count, features)
    )
    joined_part = lax.dot_general(
        grad_rows, join_pair, (((1,), (1,)), ((), ())), preferred_element_type=wide
    ).astype(narrow)
    joined_blocks = exchange(
        joined_part.reshape(dp_count, high_count * row_count, 4 * quarter * inputs), dp_axes
    )
    unit_grad = unit_kept + unit_near.astype(wide)
    own_grad, other_sent = unit_grad[:, :features], unit_grad[:, features:]

    def sum_parts(blocks):
        parts = jnp.sum(blocks.astype(wide).reshape(-1, 2, dp_count, features), axis=0)
        return parts[0] + parts[1]

    gain_high = sum_parts(grad_high[:, block_rows:])
    grad_quad = jnp.concatenate(
        [grad_high[:, :block_rows].reshape(-1, features), *split_two(gain_high)]
    )
    grad_z = gather_ring(gather_pair(grad_quad, "z_mid"), "z_lo")
    grad_z, joined_blocks, own_grad, other_sent = lax.optimization_barrier(
        (grad_z, joined_blocks, own_grad, other_sent)
    )
    grad_z = from_first(grad_z, "z_lo")
    joined_total = jnp.sum(joined_blocks.astype(wide), axis=0).astype(narrow)
    joined_high = trade_pair(
        joined_total.reshape(high_count, row_count, 4 * quarter * inputs), "z_top"
    ).reshape(high_count, row_count, 2, quarter, 2, inputs)
    joined_grad = (
        from_first(joined_high.transpose(3, 0, 1, 2, 4, 5), "z_lo")
        .transpose(2, 3, 1, 4, 0, 5)
        .reshape(row_count, 2 * z_count * inputs)
    )
    high_rows = high_count * block_rows
    gain_sum = sum_parts(grad_z[:, :, high_rows:])
    gain_grad = (gain_sum + swap_near(gain_sum)).reshape(width)
    grad_all = (
        grad_z[:, :, :high_rows]
        .reshape(quarter, 2, high_count, dp_count, row_count, features)
        .transpose(3, 2, 1, 0, 4, 5)
        .reshape(tokens, features)
    )

    other_grad = swap_cores(other_sent)
    gate_weight_grad = jnp.where(on_first, own_grad, other_grad)
    up_weight_grad = jnp.where(on_first, other_grad, own_grad)

    def add_near(sums):
        kept = lax.dynamic_index_in_dim(sums, here, 0, keepdims=False)
        sent = lax.dynamic_index_in_dim(sums, 1 - here, 0, keepdims=False)
        return kept + swap_near(sent)

    join_sums = by_core(
        jnp.dot(joined_half, grad_all, preferred_element_type=wide).reshape(2, half_inputs, features),
        jnp.dot(joined_other, grad_all, preferred_element_type=wide).reshape(2, half_inputs, features),
    )
    join_weight_grad = add_near(join_sums.transpose(1, 0, 2, 3)).reshape(inputs, features)
    return (joined_grad, gate_weight_grad, up_weight_grad, join_weight_grad, gain_grad)


def solution(mesh):
    tensor_count, dp_count = mesh.shape["tensor"], mesh.shape["dp"]
    fine = Mesh(
        mesh.devices.reshape(2, 2, 2, tensor_count // 8, dp_count // 4, 2, 2),
        ("y_lo", "z_top", "z_mid", "z_lo", "x", "y_hi", "core"),
    )
    tensor_axes = ("y_lo",) + z_axes
    dp_axes = ("x", "y_hi", "core")
    rows = P(dp_axes + tensor_axes, None)
    blocks = P(tensor_axes, dp_axes)
    in_specs = (rows, rows, rows, rows, rows, rows, P(), blocks, blocks, blocks)
    out_specs = (rows, blocks, blocks, blocks, P())
    return jax.shard_map(shards, mesh=fine, in_specs=in_specs, out_specs=out_specs, check_vma=False)
```

```python
import jax
import jax.numpy as jnp
from jax import lax
from jax.sharding import Mesh
from jax.sharding import PartitionSpec as P

epsilon = 1e-05
narrow = jnp.bfloat16
wide = jnp.float32
z_axes = ("z_hi", "z_lo")


def swiglu_back(gate_act, up_act, product_grad):
    gate_wide = gate_act.astype(wide)
    logistic = jax.nn.sigmoid(gate_wide)
    product_wide = product_grad.astype(wide)
    gate_grad = (
        product_wide * up_act.astype(wide) * logistic * (1.0 + gate_wide * (1.0 - logistic))
    )
    up_grad = product_wide * gate_wide * logistic
    return (gate_grad.astype(narrow), up_grad.astype(narrow))


def token_sum(left, right):
    return lax.dot_general(left, right, (((0,), (0,)), ((), ())), preferred_element_type=wide)


def exchange(blocks, axes):
    return lax.all_to_all(blocks, axes, split_axis=0, concat_axis=0, tiled=True)


def swap_cores(value):
    return lax.ppermute(value, "core", [(0, 1), (1, 0)])


def swap_near(value):
    return lax.ppermute(value, "y_lo", [(0, 1), (1, 0)])


def from_above(value, distance, axes=z_axes):
    count = lax.axis_size(axes)
    return lax.ppermute(value, axes, [((i + distance) % count, i) for i in range(count)])


def gather_z(block):
    z_count = lax.axis_size(z_axes)
    quarter = z_count // 4
    strided = jnp.stack([block] + [from_above(block, 4 * step) for step in range(1, quarter)])
    below = from_above(strided, z_count - 1)
    below = jnp.concatenate([below[1:], below[:1]])
    all_blocks = jnp.stack(
        [strided, from_above(strided, 1), from_above(strided, 2), below], axis=1
    ).reshape(z_count, *block.shape)
    return from_first(all_blocks, z_axes)


def gather_ring(block, axis):
    count = lax.axis_size(axis)
    return jnp.stack([block] + [from_above(block, step, axis) for step in range(1, count)])


def from_first(blocks, axes):
    twice = jnp.concatenate([blocks, blocks])
    count = blocks.shape[0]
    return lax.dynamic_slice_in_dim(twice, count - lax.axis_index(axes), count, 0)


def trade_pair(blocks, axis_name):
    first = lax.axis_index(axis_name) == 0
    kept = jnp.where(first, blocks[0], blocks[1])
    sent = jnp.where(first, blocks[1], blocks[0])
    other = lax.ppermute(sent, axis_name, [(0, 1), (1, 0)])
    return jnp.stack([jnp.where(first, kept, other), jnp.where(first, other, kept)])


def trade_x(blocks):
    count, here = lax.axis_size("x"), lax.axis_index("x")
    turned = lax.dynamic_slice_in_dim(jnp.concatenate([blocks, blocks]), here, count, 0)
    pieces = [turned[0]] + [
        lax.ppermute(turned[step], "x", [(i, (i + step) % count) for i in range(count)])
        for step in range(1, count)
    ]
    back = jnp.stack([pieces[(count - step) % count] for step in range(count)])
    return lax.dynamic_slice_in_dim(jnp.concatenate([back, back]), count - here, count, 0)


def split_three(value):
    high = value.astype(narrow)
    rest = value - high.astype(wide)
    middle = rest.astype(narrow)
    low = (rest - middle.astype(wide)).astype(narrow)
    return (high, middle, low)


def split_two(value):
    high = value.astype(narrow)
    return (high, (value - high.astype(wide)).astype(narrow))


def shards(
    hidden,
    joined_in,
    gate_act,
    up_act,
    product_grad,
    resid_grad,
    norm_gain,
    gate_weight,
    up_weight,
    join_weight,
):
    dp_axes = ("x", "y_hi", "core")
    quarter = lax.axis_size("z_lo")
    z_count = lax.axis_size("z_hi") * quarter
    core_count = lax.axis_size("core")
    dp_count = lax.axis_size("x") * lax.axis_size("y_hi") * core_count
    row_count, width = hidden.shape
    units, features = gate_weight.shape
    inputs = join_weight.shape[0]
    half_inputs = inputs // 2
    part_width = units + half_inputs
    plane_rows = z_count * row_count
    block_rows = dp_count * row_count
    tokens = dp_count * plane_rows
    on_first = lax.axis_index("core") == 0
    here = lax.axis_index("y_lo")
    near_first = here == 0

    def by_near(own, near):
        return jnp.stack([jnp.where(near_first, own, near), jnp.where(near_first, near, own)])

    def by_core(own, other):
        return jnp.stack([jnp.where(on_first, own, other), jnp.where(on_first, other, own)])

    gate_grad, up_grad = swiglu_back(gate_act, up_act, product_grad)
    joined_rows = joined_in.reshape(row_count, 2, z_count, 2, half_inputs)
    gate_rows = jnp.concatenate(
        [gate_grad.reshape(row_count, 2, z_count, units), joined_rows[:, :, :, 0]], axis=3
    )
    up_rows = jnp.concatenate(
        [up_grad.reshape(row_count, 2, z_count, units), joined_rows[:, :, :, 1]], axis=3
    )
    unit_rows = jnp.stack([gate_rows, up_rows]).transpose(3, 0, 1, 2, 4)
    unit_rows = unit_rows.reshape(z_count, 2 * row_count, 2 * part_width)
    unit_rows, hidden, resid_grad = lax.optimization_barrier((unit_rows, hidden, resid_grad))
    unit_group = exchange(unit_rows, z_axes)

    hidden_wide = hidden.astype(wide)
    row_scale = lax.rsqrt(jnp.mean(hidden_wide * hidden_wide, axis=1, keepdims=True) + epsilon)
    scale_parts = jnp.concatenate(split_three(row_scale), axis=1)
    scale_parts = jnp.pad(scale_parts, ((0, 0), (0, features - scale_parts.shape[1])))
    norm_rows = jnp.stack(
        [
            hidden.reshape(row_count, dp_count, features),
            resid_grad.reshape(row_count, dp_count, features),
            jnp.broadcast_to(scale_parts[:, None, :], (row_count, dp_count, features)),
        ]
    )
    norm_sent = norm_rows.transpose(2, 0, 1, 3).reshape(
        lax.axis_size("x"), 2, 2, 3 * row_count, features
    )
    norm_block = trade_pair(norm_sent.transpose(2, 0, 1, 3, 4), "core")
    norm_block, near_weights = lax.optimization_barrier(
        (norm_block, swap_near(jnp.stack([gate_weight, up_weight])))
    )
    near_gate, near_up = near_weights[0], near_weights[1]
    norm_block = trade_pair(norm_block.transpose(2, 0, 1, 3, 4), "y_hi")
    norm_block = trade_x(norm_block.transpose(2, 0, 1, 3, 4)).reshape(
        dp_count, 3, row_count, features
    )
    hidden_block = norm_block[:, 0].reshape(block_rows, features).astype(wide)
    resid_block = norm_block[:, 1].reshape(block_rows, features).astype(wide)
    scale_block = norm_block[:, 2, :, :3].astype(wide).reshape(block_rows, 3)
    scale_block = (scale_block[:, 0:1] + scale_block[:, 1:2]) + scale_block[:, 2:3]
    gain_block = lax.dynamic_slice_in_dim(
        norm_gain, lax.axis_index(dp_axes) * features, features, 0
    )
    normed = hidden_block * scale_block
    mlp_block = (normed * gain_block).astype(narrow)

    unit_group, mlp_block = lax.optimization_barrier((unit_group, mlp_block))
    mlp_z = gather_z(mlp_block)
    unit_halves = (
        unit_group.reshape(z_count, 2, row_count, 2 * part_width)
        .transpose(1, 0, 2, 3)
        .reshape(2, plane_rows, 2 * part_width)
    )
    unit_halves = jnp.broadcast_to(
        unit_halves[None], (dp_count // core_count, core_count, plane_rows, 2 * part_width)
    ).reshape(dp_count, plane_rows, 2 * part_width)
    half_all = exchange(unit_halves, dp_axes).reshape(tokens, 2 * part_width)
    join_quad = gather_ring(join_weight, "z_lo")
    half_all, mlp_z, join_quad = lax.optimization_barrier((half_all, mlp_z, join_quad))

    def both_near(own, near):
        both = jnp.pad(by_near(own, near), ((0, 0), (0, half_inputs), (0, 0)))
        return both.reshape(2 * part_width, features)

    weight_own = both_near(
        jnp.where(on_first, gate_weight, up_weight), jnp.where(on_first, near_gate, near_up)
    )
    weight_other = swap_cores(
        both_near(
            jnp.where(on_first, up_weight, gate_weight), jnp.where(on_first, near_up, near_gate)
        )
    )
    partial_other = jnp.dot(half_all, weight_other, preferred_element_type=wide)
    partial_own = jnp.dot(half_all, weight_own, preferred_element_type=wide)
    partial_value = partial_own + swap_cores(partial_other)
    partial_value = (
        partial_value.astype(narrow)
        .reshape(dp_count, z_count, row_count, features)
        .transpose(1, 0, 2, 3)
        .reshape(z_count, block_rows, features)
    )

    mlp_own = (
        mlp_z.reshape(z_count, dp_count, row_count, features)
        .transpose(1, 0, 2, 3)
        .reshape(tokens, features)
    )
    unit_sums = token_sum(half_all, jnp.concatenate([mlp_own, swap_cores(mlp_own)], axis=1))
    unit_sums = unit_sums.reshape(2, part_width, 2 * features)[:, :units]
    unit_kept = lax.dynamic_index_in_dim(unit_sums, here, 0, keepdims=False)
    unit_sent = lax.dynamic_index_in_dim(unit_sums, 1 - here, 0, keepdims=False)
    joined_half = jnp.concatenate(
        [half_all[:, units:part_width], half_all[:, part_width + units :]], axis=1
    )
    partial_far, unit_sent, joined_half, joined_other, near_quad = lax.optimization_barrier(
        (
            exchange(partial_value, z_axes),
            unit_sent.astype(narrow),
            joined_half,
            swap_cores(joined_half),
            swap_near(join_quad),
        )
    )
    unit_near = swap_near(unit_sent)
    input_grad = jnp.sum(partial_far.astype(wide), axis=0)

    lifted = input_grad * gain_block
    mean_part = jnp.sum(lifted * normed, axis=1)
    gain_part = jnp.sum(input_grad * normed, axis=0)
    row_parts = jnp.concatenate([mean_part, gain_part])
    row_parts = exchange(
        jnp.broadcast_to(row_parts[None, None], (dp_count, 1, block_rows + features)), dp_axes
    )[:, 0]
    inner_mean = (jnp.sum(row_parts[:, :block_rows], axis=0) / width)[:, None]
    gain_part = row_parts[:, block_rows:]
    hidden_grad = (resid_block + scale_block * (lifted - normed * inner_mean)).astype(narrow)

    grad_sent = jnp.concatenate([hidden_grad, *split_two(gain_part)])
    sent_rows = block_rows + 2 * dp_count
    high_count = z_count // quarter
    grad_high = exchange(
        jnp.broadcast_to(grad_sent[None], (high_count, sent_rows, features)), "z_hi"
    )

    join_pair = by_near(join_quad, near_quad).reshape(2 * quarter * inputs, features)
    joined_half, joined_other = joined_half.T, joined_other.T
    unit_grad = unit_kept + unit_near.astype(wide)
    grad_high, own_grad, other_sent, join_pair, joined_half, joined_other = (
        lax.optimization_barrier(
            (
                grad_high,
                unit_grad[:, :features],
                unit_grad[:, features:],
                join_pair,
                joined_half,
                joined_other,
            )
        )
    )

    grad_rows = (
        grad_high[:, :block_rows]
        .reshape(high_count, dp_count, row_count, features)
        .transpose(1, 0, 2, 3)
        .reshape(dp_count * high_count * row_count, features)
    )
    joined_part = lax.dot_general(
        grad_rows, join_pair, (((1,), (1,)), ((), ())), preferred_element_type=wide
    ).astype(narrow)
    joined_blocks = exchange(
        joined_part.reshape(dp_count, high_count * row_count, 2 * quarter * inputs), dp_axes
    )
    grad_high, other_grad = lax.optimization_barrier((grad_high, swap_cores(other_sent)))
    gate_weight_grad = jnp.where(on_first, own_grad, other_grad)
    up_weight_grad = jnp.where(on_first, other_grad, own_grad)

    def sum_parts(blocks):
        parts = jnp.sum(blocks.astype(wide).reshape(-1, 2, dp_count, features), axis=0)
        return parts[0] + parts[1]

    gain_high = sum_parts(grad_high[:, block_rows:])
    grad_quad = jnp.concatenate(
        [grad_high[:, :block_rows].reshape(-1, features), *split_two(gain_high)]
    )
    grad_z = from_first(gather_ring(grad_quad, "z_lo"), "z_lo")
    joined_total = jnp.sum(joined_blocks.astype(wide), axis=0).astype(narrow)
    joined_high = exchange(
        joined_total.reshape(high_count, row_count, 2 * quarter * inputs), "z_hi"
    ).reshape(high_count, row_count, 2, quarter, inputs)
    joined_grad = (
        from_first(joined_high.transpose(3, 0, 1, 2, 4), "z_lo")
        .transpose(2, 3, 1, 0, 4)
        .reshape(row_count, 2 * z_count * inputs)
    )

    high_rows = high_count * block_rows
    gain_sum = sum_parts(grad_z[:, high_rows:])
    gain_grad = (gain_sum + swap_near(gain_sum)).reshape(width)
    grad_all = (
        grad_z[:, :high_rows]
        .reshape(quarter, high_count, dp_count, row_count, features)
        .transpose(2, 1, 0, 3, 4)
        .reshape(tokens, features)
    )

    def add_near(sums):
        kept = lax.dynamic_index_in_dim(sums, here, 0, keepdims=False)
        sent = lax.dynamic_index_in_dim(sums, 1 - here, 0, keepdims=False)
        return kept + swap_near(sent)

    join_sums = by_core(
        jnp.dot(joined_half, grad_all, preferred_element_type=wide).reshape(2, half_inputs, features),
        jnp.dot(joined_other, grad_all, preferred_element_type=wide).reshape(2, half_inputs, features),
    )
    join_weight_grad = add_near(join_sums.transpose(1, 0, 2, 3)).reshape(inputs, features)
    return (joined_grad, gate_weight_grad, up_weight_grad, join_weight_grad, gain_grad)


def solution(mesh):
    tensor_count, dp_count = mesh.shape["tensor"], mesh.shape["dp"]
    fine = Mesh(
        mesh.devices.reshape(2, tensor_count // 8, 4, dp_count // 4, 2, 2),
        ("y_lo", "z_hi", "z_lo", "x", "y_hi", "core"),
    )
    tensor_axes = ("y_lo",) + z_axes
    dp_axes = ("x", "y_hi", "core")
    rows = P(dp_axes + tensor_axes, None)
    blocks = P(tensor_axes, dp_axes)
    in_specs = (rows, rows, rows, rows, rows, rows, P(), blocks, blocks, blocks)
    out_specs = (rows, blocks, blocks, blocks, P())
    return jax.shard_map(shards, mesh=fine, in_specs=in_specs, out_specs=out_specs, check_vma=False)
```

```python
import jax
import jax.numpy as jnp
from jax import lax
from jax.sharding import Mesh
from jax.sharding import PartitionSpec as P

epsilon = 1e-05
narrow = jnp.bfloat16
wide = jnp.float32
z_axes = ("z_hi", "z_lo")


def swiglu_back(gate_act, up_act, product_grad):
    gate_wide = gate_act.astype(wide)
    logistic = jax.nn.sigmoid(gate_wide)
    product_wide = product_grad.astype(wide)
    gate_grad = (
        product_wide * up_act.astype(wide) * logistic * (1.0 + gate_wide * (1.0 - logistic))
    )
    up_grad = product_wide * gate_wide * logistic
    return (gate_grad.astype(narrow), up_grad.astype(narrow))


def token_sum(left, right):
    return lax.dot_general(left, right, (((0,), (0,)), ((), ())), preferred_element_type=wide)


def exchange(blocks, axes):
    return lax.all_to_all(blocks, axes, split_axis=0, concat_axis=0, tiled=True)


def swap_cores(value):
    return lax.ppermute(value, "core", [(0, 1), (1, 0)])


def swap_near(value):
    return lax.ppermute(value, "y_lo", [(0, 1), (1, 0)])


def from_above(value, distance, axes=z_axes):
    count = lax.axis_size(axes)
    return lax.ppermute(value, axes, [((i + distance) % count, i) for i in range(count)])


def gather_z(block):
    z_count = lax.axis_size(z_axes)
    quarter = z_count // 4
    strided = jnp.stack([block] + [from_above(block, 4 * step) for step in range(1, quarter)])
    below = from_above(strided, z_count - 1)
    below = jnp.concatenate([below[1:], below[:1]])
    all_blocks = jnp.stack(
        [strided, from_above(strided, 1), from_above(strided, 2), below], axis=1
    ).reshape(z_count, *block.shape)
    return from_first(all_blocks, z_axes)


def gather_ring(block, axis):
    count = lax.axis_size(axis)
    return jnp.stack([block] + [from_above(block, step, axis) for step in range(1, count)])


def from_first(blocks, axes):
    twice = jnp.concatenate([blocks, blocks])
    count = blocks.shape[0]
    return lax.dynamic_slice_in_dim(twice, count - lax.axis_index(axes), count, 0)


def trade_pair(blocks, axis_name):
    first = lax.axis_index(axis_name) == 0
    kept = jnp.where(first, blocks[0], blocks[1])
    sent = jnp.where(first, blocks[1], blocks[0])
    other = lax.ppermute(sent, axis_name, [(0, 1), (1, 0)])
    return jnp.stack([jnp.where(first, kept, other), jnp.where(first, other, kept)])


def trade_x(blocks):
    count, here = lax.axis_size("x"), lax.axis_index("x")
    turned = lax.dynamic_slice_in_dim(jnp.concatenate([blocks, blocks]), here, count, 0)
    pieces = [turned[0]] + [
        lax.ppermute(turned[step], "x", [(i, (i + step) % count) for i in range(count)])
        for step in range(1, count)
    ]
    back = jnp.stack([pieces[(count - step) % count] for step in range(count)])
    return lax.dynamic_slice_in_dim(jnp.concatenate([back, back]), count - here, count, 0)


def split_three(value):
    high = value.astype(narrow)
    rest = value - high.astype(wide)
    middle = rest.astype(narrow)
    low = (rest - middle.astype(wide)).astype(narrow)
    return (high, middle, low)


def split_two(value):
    high = value.astype(narrow)
    return (high, (value - high.astype(wide)).astype(narrow))


def shards(
    hidden,
    joined_in,
    gate_act,
    up_act,
    product_grad,
    resid_grad,
    norm_gain,
    gate_weight,
    up_weight,
    join_weight,
):
    dp_axes = ("x", "y_hi", "core")
    quarter = lax.axis_size("z_lo")
    z_count = lax.axis_size("z_hi") * quarter
    core_count = lax.axis_size("core")
    dp_count = lax.axis_size("x") * lax.axis_size("y_hi") * core_count
    row_count, width = hidden.shape
    units, features = gate_weight.shape
    inputs = join_weight.shape[0]
    half_inputs = inputs // 2
    part_width = units + half_inputs
    plane_rows = z_count * row_count
    block_rows = dp_count * row_count
    tokens = dp_count * plane_rows
    on_first = lax.axis_index("core") == 0
    here = lax.axis_index("y_lo")
    near_first = here == 0

    def by_near(own, near):
        return jnp.stack([jnp.where(near_first, own, near), jnp.where(near_first, near, own)])

    def by_core(own, other):
        return jnp.stack([jnp.where(on_first, own, other), jnp.where(on_first, other, own)])

    gate_grad, up_grad = swiglu_back(gate_act, up_act, product_grad)
    joined_rows = joined_in.reshape(row_count, 2, z_count, 2, half_inputs)
    gate_rows = jnp.concatenate(
        [gate_grad.reshape(row_count, 2, z_count, units), joined_rows[:, :, :, 0]], axis=3
    )
    up_rows = jnp.concatenate(
        [up_grad.reshape(row_count, 2, z_count, units), joined_rows[:, :, :, 1]], axis=3
    )
    unit_rows = jnp.stack([gate_rows, up_rows]).transpose(3, 0, 1, 2, 4)
    unit_rows = unit_rows.reshape(z_count, 2 * row_count, 2 * part_width)
    unit_rows, hidden, resid_grad = lax.optimization_barrier((unit_rows, hidden, resid_grad))
    unit_group = exchange(unit_rows, z_axes)

    hidden_wide = hidden.astype(wide)
    row_scale = lax.rsqrt(jnp.mean(hidden_wide * hidden_wide, axis=1, keepdims=True) + epsilon)
    scale_parts = jnp.concatenate(split_three(row_scale), axis=1)
    scale_parts = jnp.pad(scale_parts, ((0, 0), (0, features - scale_parts.shape[1])))
    norm_rows = jnp.stack(
        [
            hidden.reshape(row_count, dp_count, features),
            resid_grad.reshape(row_count, dp_count, features),
            jnp.broadcast_to(scale_parts[:, None, :], (row_count, dp_count, features)),
        ]
    )
    norm_sent = norm_rows.transpose(2, 0, 1, 3).reshape(
        lax.axis_size("x"), 2, 2, 3 * row_count, features
    )
    norm_block = trade_pair(norm_sent.transpose(2, 0, 1, 3, 4), "core")
    norm_block, near_weights = lax.optimization_barrier(
        (norm_block, swap_near(jnp.stack([gate_weight, up_weight])))
    )
    near_gate, near_up = near_weights[0], near_weights[1]
    norm_block = trade_pair(norm_block.transpose(2, 0, 1, 3, 4), "y_hi")
    norm_block = trade_x(norm_block.transpose(2, 0, 1, 3, 4)).reshape(
        dp_count, 3, row_count, features
    )
    hidden_block = norm_block[:, 0].reshape(block_rows, features).astype(wide)
    resid_block = norm_block[:, 1].reshape(block_rows, features).astype(wide)
    scale_block = norm_block[:, 2, :, :3].astype(wide).reshape(block_rows, 3)
    scale_block = (scale_block[:, 0:1] + scale_block[:, 1:2]) + scale_block[:, 2:3]
    gain_block = lax.dynamic_slice_in_dim(
        norm_gain, lax.axis_index(dp_axes) * features, features, 0
    )
    normed = hidden_block * scale_block
    mlp_block = (normed * gain_block).astype(narrow)

    unit_group, mlp_block = lax.optimization_barrier((unit_group, mlp_block))
    mlp_z = gather_z(mlp_block)
    unit_halves = (
        unit_group.reshape(z_count, 2, row_count, 2 * part_width)
        .transpose(1, 0, 2, 3)
        .reshape(2, plane_rows, 2 * part_width)
    )
    unit_halves = jnp.broadcast_to(
        unit_halves[None], (dp_count // core_count, core_count, plane_rows, 2 * part_width)
    ).reshape(dp_count, plane_rows, 2 * part_width)
    half_all = exchange(unit_halves, dp_axes).reshape(tokens, 2 * part_width)
    join_quad = gather_ring(join_weight, "z_lo")
    half_all, mlp_z, join_quad = lax.optimization_barrier((half_all, mlp_z, join_quad))

    def both_near(own, near):
        both = jnp.pad(by_near(own, near), ((0, 0), (0, half_inputs), (0, 0)))
        return both.reshape(2 * part_width, features)

    weight_own = both_near(
        jnp.where(on_first, gate_weight, up_weight), jnp.where(on_first, near_gate, near_up)
    )
    weight_other = swap_cores(
        both_near(
            jnp.where(on_first, up_weight, gate_weight), jnp.where(on_first, near_up, near_gate)
        )
    )
    partial_other = jnp.dot(half_all, weight_other, preferred_element_type=wide)
    partial_own = jnp.dot(half_all, weight_own, preferred_element_type=wide)
    partial_value = partial_own + swap_cores(partial_other)
    partial_value = (
        partial_value.astype(narrow)
        .reshape(dp_count, z_count, row_count, features)
        .transpose(1, 0, 2, 3)
        .reshape(z_count, block_rows, features)
    )

    mlp_own = (
        mlp_z.reshape(z_count, dp_count, row_count, features)
        .transpose(1, 0, 2, 3)
        .reshape(tokens, features)
    )
    unit_sums = token_sum(half_all, jnp.concatenate([mlp_own, swap_cores(mlp_own)], axis=1))
    unit_sums = unit_sums.reshape(2, part_width, 2 * features)[:, :units]
    unit_kept = lax.dynamic_index_in_dim(unit_sums, here, 0, keepdims=False)
    unit_sent = lax.dynamic_index_in_dim(unit_sums, 1 - here, 0, keepdims=False)
    joined_half = jnp.concatenate(
        [half_all[:, units:part_width], half_all[:, part_width + units :]], axis=1
    )
    joined_half = joined_half.reshape(-1, quarter, row_count, inputs)
    joined_half = lax.dynamic_slice_in_dim(
        jnp.concatenate([joined_half, joined_half], axis=1), lax.axis_index("z_lo"), quarter, 1
    ).reshape(tokens, inputs)
    partial_far, unit_sent, joined_half, joined_other, near_quad = lax.optimization_barrier(
        (
            exchange(partial_value, z_axes),
            unit_sent.astype(narrow),
            joined_half,
            swap_cores(joined_half),
            swap_near(join_quad),
        )
    )
    unit_near = swap_near(unit_sent)
    input_grad = jnp.sum(partial_far.astype(wide), axis=0)

    lifted = input_grad * gain_block
    mean_part = jnp.sum(lifted * normed, axis=1)
    gain_part = jnp.sum(input_grad * normed, axis=0)
    row_parts = jnp.concatenate([mean_part, gain_part])
    row_parts = exchange(
        jnp.broadcast_to(row_parts[None, None], (dp_count, 1, block_rows + features)), dp_axes
    )[:, 0]
    inner_mean = (jnp.sum(row_parts[:, :block_rows], axis=0) / width)[:, None]
    gain_part = row_parts[:, block_rows:]
    hidden_grad = (resid_block + scale_block * (lifted - normed * inner_mean)).astype(narrow)

    grad_sent = jnp.concatenate([hidden_grad, *split_two(gain_part)])
    sent_rows = block_rows + 2 * dp_count
    high_count = z_count // quarter
    grad_high = exchange(
        jnp.broadcast_to(grad_sent[None], (high_count, sent_rows, features)), "z_hi"
    )

    join_pair = by_near(join_quad, near_quad).reshape(2 * quarter * inputs, features)
    joined_half, joined_other = joined_half.T, joined_other.T
    unit_grad = unit_kept + unit_near.astype(wide)
    grad_high, own_grad, other_sent, join_pair, joined_half, joined_other = (
        lax.optimization_barrier(
            (
                grad_high,
                unit_grad[:, :features],
                unit_grad[:, features:],
                join_pair,
                joined_half,
                joined_other,
            )
        )
    )

    grad_rows = (
        grad_high[:, :block_rows]
        .reshape(high_count, dp_count, row_count, features)
        .transpose(1, 0, 2, 3)
        .reshape(dp_count * high_count * row_count, features)
    )
    joined_part = lax.dot_general(
        grad_rows, join_pair, (((1,), (1,)), ((), ())), preferred_element_type=wide
    ).astype(narrow)
    joined_blocks = exchange(
        joined_part.reshape(dp_count, high_count * row_count, 2 * quarter * inputs), dp_axes
    )
    grad_high, other_grad = lax.optimization_barrier((grad_high, swap_cores(other_sent)))
    gate_weight_grad = jnp.where(on_first, own_grad, other_grad)
    up_weight_grad = jnp.where(on_first, other_grad, own_grad)

    def sum_parts(blocks):
        parts = jnp.sum(blocks.astype(wide).reshape(-1, 2, dp_count, features), axis=0)
        return parts[0] + parts[1]

    gain_high = sum_parts(grad_high[:, block_rows:])
    grad_quad = jnp.concatenate(
        [grad_high[:, :block_rows].reshape(-1, features), *split_two(gain_high)]
    )
    grad_z = gather_ring(grad_quad, "z_lo")
    joined_total = jnp.sum(joined_blocks.astype(wide), axis=0).astype(narrow)
    joined_high = exchange(
        joined_total.reshape(high_count, row_count, 2 * quarter * inputs), "z_hi"
    ).reshape(high_count, row_count, 2, quarter, inputs)
    joined_grad = (
        from_first(joined_high.transpose(3, 0, 1, 2, 4), "z_lo")
        .transpose(2, 3, 1, 0, 4)
        .reshape(row_count, 2 * z_count * inputs)
    )

    high_rows = high_count * block_rows
    gain_sum = sum_parts(from_first(grad_z[:, high_rows:], "z_lo"))
    gain_grad = (gain_sum + swap_near(gain_sum)).reshape(width)
    grad_all = (
        grad_z[:, :high_rows]
        .reshape(quarter, high_count, dp_count, row_count, features)
        .transpose(2, 1, 0, 3, 4)
        .reshape(tokens, features)
    )

    def add_near(sums):
        kept = lax.dynamic_index_in_dim(sums, here, 0, keepdims=False)
        sent = lax.dynamic_index_in_dim(sums, 1 - here, 0, keepdims=False)
        return kept + swap_near(sent)

    join_sums = by_core(
        jnp.dot(joined_half, grad_all, preferred_element_type=wide).reshape(2, half_inputs, features),
        jnp.dot(joined_other, grad_all, preferred_element_type=wide).reshape(2, half_inputs, features),
    )
    join_weight_grad = add_near(join_sums.transpose(1, 0, 2, 3)).reshape(inputs, features)
    return (joined_grad, gate_weight_grad, up_weight_grad, join_weight_grad, gain_grad)


def solution(mesh):
    tensor_count, dp_count = mesh.shape["tensor"], mesh.shape["dp"]
    fine = Mesh(
        mesh.devices.reshape(2, tensor_count // 8, 4, dp_count // 4, 2, 2),
        ("y_lo", "z_hi", "z_lo", "x", "y_hi", "core"),
    )
    tensor_axes = ("y_lo",) + z_axes
    dp_axes = ("x", "y_hi", "core")
    rows = P(dp_axes + tensor_axes, None)
    blocks = P(tensor_axes, dp_axes)
    in_specs = (rows, rows, rows, rows, rows, rows, P(), blocks, blocks, blocks)
    out_specs = (rows, blocks, blocks, blocks, P())
    return jax.shard_map(shards, mesh=fine, in_specs=in_specs, out_specs=out_specs, check_vma=False)
```
